512 devices in a mesh: mem: 64 (over x, y, core), tile: 8 (over z).
Axes of the slice: x: 4, y: 8, z: 8, core: 2. Of those that a mesh axis runs over, the one named last changes fastest.
Arguments:
- background_members: bfloat16 [64, 2, 256, 4096], P('mem', None, None, 'tile'), may hold values from -6 to 6
- measured_datum: float32 [2, 64, 8, 64], P(None, 'mem', 'tile'), may hold values from -12 to 12
- measurement_noise_spread: float32 [2, 64, 8, 64], P(None, 'mem', 'tile'), may hold values from 0.1 to 2
- measured_point: int32 [2, 64, 8, 64], P(None, 'mem', 'tile'), may hold values from 0 to 4095
- active_measure_total: int32 [2, 64, 8], P(None, 'mem', 'tile'), may hold values from 1 to 64, as said below
Outputs:
- analysis: bfloat16 [64, 2, 256, 4096], P('mem', None, None, 'tile')
The draws below stay inside these ranges and needn't reach their ends.
Inputs may be any that keep to these rules, and one draw needn't show every extreme that they name: `measured_point`: cell number within the owning tile, level * 4 * 512 + row in tile * 512 + column in tile. `active_measure_total`: slots from this count on are not live; in every batch some tile has all 64 slots live.
All inputs are finite; a program needn't handle non-finite values.
Results may differ from the reference program's by a relative error of at most 0.001.
Values may be sent and summed in bfloat16 or wider, within the bound.
No kernel may reach another device: no remote copies, remote signals or barrier semaphores. Data moves between devices by JAX's collectives and lax.ppermute only.
A program may use at most 64 MiB of HBM per device.

```python
import math
import jax
import jax.numpy as jnp
from jax import lax

MEMBER_TOTAL = 64
VERTICAL_LAYERS = 2
PATCH_SPAN_NORTH = 4
PATCH_SPAN_EAST = 512
OBS_TILE = 64
NB = 2
PATCH_NORTHWARD = 64
PATCH_EASTWARD = 8
MESH_NORTHWARD = 256
MESH_EASTWARD = 4096


def draw_active_measure_total(key, part):
    key = jax.random.fold_in(key, 7)
    first_key, second_key, third_key = jax.random.split(key, 3)
    first = jax.random.randint(first_key, (NB, PATCH_NORTHWARD, PATCH_EASTWARD), 1, OBS_TILE + 1)
    second = jax.random.randint(second_key, (NB, PATCH_NORTHWARD, PATCH_EASTWARD), 1, OBS_TILE + 1)
    chosen = jax.random.randint(third_key, (NB, 1, 1), 0, PATCH_NORTHWARD * PATCH_EASTWARD)
    position = jnp.arange(PATCH_NORTHWARD * PATCH_EASTWARD, dtype=jnp.int32).reshape(1, PATCH_NORTHWARD, PATCH_EASTWARD)
    return jnp.where(position == chosen, OBS_TILE, jnp.minimum(first, second)).astype(jnp.int32)


def touch_ends(result, key, low, largest):
    shape = result.shape
    place = [jax.random.randint(jax.random.fold_in(key, axis), (), 0, shape[axis]) for axis in range(len(shape))]
    result = result.at[tuple(place)].set(low)
    longest = shape.index(max(shape))
    place[longest] = (place[longest] + 1) % shape[longest]
    return result.at[tuple(place)].set(largest)


def level_of(rng, dims, shards, least, largest):
    def one(axis_at, blocks):
        heights = jax.random.uniform(jax.random.fold_in(jax.random.fold_in(rng, 6), axis_at), (blocks,), jnp.float32, least / len(shards), largest / len(shards))
        return jnp.repeat(jnp.exp(heights), dims[axis_at] // blocks).reshape((-1,) + (1,) * (len(dims) - axis_at - 1))

    gain = one(*shards[0])
    for cut in shards[1:]:
        gain = gain * one(*cut)
    return gain


def scatter_about(own_key, shape, spread, most, pieces=(), kind=jnp.bfloat16):
    result = jax.random.normal(own_key, shape, jnp.float32) * spread
    if len(pieces) > 0:
        result = level_of(own_key, shape, pieces, -0.22, 0.18) * result
    return jnp.clip(result, min=-most, max=most).astype(kind)


def setup_inputs(seed: int = 0) -> dict:
    arg_keys = jax.random.split(jax.random.key(seed), 6)
    return {
        "background_members": scatter_about(arg_keys[0], (MEMBER_TOTAL, VERTICAL_LAYERS, MESH_NORTHWARD, MESH_EASTWARD), 1.0, 6.0, ((0, 64), (3, 8))),
        "measured_datum": scatter_about(arg_keys[1], (NB, PATCH_NORTHWARD, PATCH_EASTWARD, OBS_TILE), 2.0, 12.0, ((1, 64), (2, 8)), jnp.float32),
        "measurement_noise_spread": jnp.clip(jnp.exp(math.log(2.0) - 2.9957323 * jax.random.uniform(arg_keys[2], (NB, PATCH_NORTHWARD, PATCH_EASTWARD, OBS_TILE), jnp.float32) ** level_of(arg_keys[2], (NB, PATCH_NORTHWARD, PATCH_EASTWARD, OBS_TILE), ((1, 64), (2, 8)), -0.2, 0.2)), 0.1, 2.0),
        "measured_point": touch_ends(jax.random.randint(arg_keys[3], (NB, PATCH_NORTHWARD, PATCH_EASTWARD, OBS_TILE), 0, VERTICAL_LAYERS * PATCH_SPAN_NORTH * PATCH_SPAN_EAST), jax.random.fold_in(arg_keys[3], 1), 0, (VERTICAL_LAYERS * PATCH_SPAN_NORTH * PATCH_SPAN_EAST) - 1).astype(jnp.int32),
        "active_measure_total": draw_active_measure_total(jax.random.fold_in(arg_keys[5], 71), 0),
    }


def gaspari(distance, cutoff):
    scaled = distance / (0.5 * cutoff)
    clipped = jnp.maximum(scaled, 1.0)
    inside_part = (((-0.25 * scaled + 0.5) * scaled + 0.625) * scaled - 5.0 / 3.0) * scaled * scaled + 1.0
    outside_part = ((((scaled / 12.0 - 0.5) * scaled + 0.625) * scaled + 5.0 / 3.0) * scaled - 5.0) * scaled + 4.0 - 2.0 / (3.0 * clipped)
    return jnp.where(scaled <= 1.0, inside_part, jnp.where(scaled < 2.0, outside_part, jnp.zeros_like(scaled)))

def make_packet(columns, obs_values, error_var, live_count, site_ids):
    prior_mean = lax.optimization_barrier(jnp.mean(columns, axis=0))
    prior_pert = columns - prior_mean
    variance = lax.optimization_barrier(jnp.sum(prior_pert * prior_pert, axis=0)) / (MEMBER_TOTAL - 1)
    denominator = variance + error_var
    live_mask = (jnp.arange(columns.shape[1], dtype=jnp.int32) < live_count).astype(columns.dtype)
    factor = 1.0 / (1.0 + jnp.sqrt(error_var / denominator))
    mean_weight = live_mask * (obs_values - prior_mean) / denominator
    pert_weight = live_mask * factor / denominator
    return jnp.concatenate([prior_pert, mean_weight[None], pert_weight[None], site_ids.astype(columns.dtype)[None]], axis=0)

def unpack(neighbours):
    slots = neighbours.shape[3]
    flattened = jnp.transpose(neighbours.reshape(9, MEMBER_TOTAL + 3, slots), (1, 0, 2)).reshape(MEMBER_TOTAL + 3, 9 * slots)
    perturb = flattened[:MEMBER_TOTAL]
    site_ids = flattened[MEMBER_TOTAL + 2].astype(jnp.int32)
    slot_of = jnp.arange(9 * slots, dtype=jnp.int32) // slots
    row_shift = slot_of // 3 - 1
    col_shift = slot_of % 3 - 1
    obs_row = (row_shift * PATCH_SPAN_NORTH + site_ids % (PATCH_SPAN_NORTH * PATCH_SPAN_EAST) // PATCH_SPAN_EAST).astype(perturb.dtype)
    obs_col = (col_shift * PATCH_SPAN_EAST + site_ids % PATCH_SPAN_EAST).astype(perturb.dtype)
    obs_level = (site_ids // (PATCH_SPAN_NORTH * PATCH_SPAN_EAST)).astype(perturb.dtype)
    return (perturb, flattened[MEMBER_TOTAL], flattened[MEMBER_TOTAL + 1], obs_row, obs_col, obs_level)

def update_block(block_state, cell_ids, unpacked):
    perturb, mean_weight, pert_weight, obs_row, obs_col, obs_level = unpacked
    kind = block_state.dtype
    cell_mean = lax.optimization_barrier(jnp.mean(block_state, axis=0))
    cell_pert = block_state - cell_mean
    covariance = lax.dot_general(perturb, cell_pert, (((0,), (0,)), ((), ())), precision=lax.Precision.HIGHEST) / (MEMBER_TOTAL - 1)
    cell_level = (cell_ids // (PATCH_SPAN_NORTH * PATCH_SPAN_EAST)).astype(kind)
    cell_row = (cell_ids % (PATCH_SPAN_NORTH * PATCH_SPAN_EAST) // PATCH_SPAN_EAST).astype(kind)
    cell_col = (cell_ids % PATCH_SPAN_EAST).astype(kind)
    row_gap = obs_row[:, None] - cell_row[None, :]
    col_gap = obs_col[:, None] - cell_col[None, :]
    distance = jnp.sqrt(row_gap * row_gap + col_gap * col_gap)
    weight = gaspari(distance, 2 * PATCH_SPAN_NORTH) / (1.0 + jnp.abs(obs_level[:, None] - cell_level[None, :]))
    gain_terms = weight * covariance
    mean_step = jnp.dot(mean_weight[None, :], gain_terms, precision=lax.Precision.HIGHEST)[0]
    pert_step = jnp.dot(perturb, gain_terms * pert_weight[:, None], precision=lax.Precision.HIGHEST)
    return cell_mean + mean_step + cell_pert - pert_step

def tile_update(member_fields, unpacked):
    cell_total = member_fields.shape[1]
    width = math.gcd(cell_total, 128)
    blocks = jnp.transpose(member_fields.reshape(MEMBER_TOTAL, cell_total // width, width), (1, 0, 2))
    cell_ids = jnp.arange(cell_total, dtype=jnp.int32).reshape(cell_total // width, width)
    updated = lax.map(lambda operands: update_block(operands[0], operands[1], unpacked), (blocks, cell_ids))
    return jnp.transpose(updated, (1, 0, 2)).reshape(MEMBER_TOTAL, cell_total)

def reference(background_members, measured_datum, measurement_noise_spread, measured_point, active_measure_total):
    cell_total = VERTICAL_LAYERS * PATCH_SPAN_NORTH * PATCH_SPAN_EAST
    member_fields = background_members.astype(jnp.float32).reshape(MEMBER_TOTAL, VERTICAL_LAYERS, PATCH_NORTHWARD, PATCH_SPAN_NORTH, PATCH_EASTWARD, PATCH_SPAN_EAST)
    member_fields = jnp.transpose(member_fields, (2, 4, 0, 1, 3, 5)).reshape(PATCH_NORTHWARD * PATCH_EASTWARD, MEMBER_TOTAL, cell_total)
    for batch_index in range(NB):
        site_ids = measured_point[batch_index].reshape(PATCH_NORTHWARD * PATCH_EASTWARD, OBS_TILE)
        columns = jax.vmap(lambda patch_field_block, picks: jnp.take(patch_field_block, picks, axis=1))(member_fields, site_ids)
        packets = jax.vmap(make_packet)(columns, measured_datum[batch_index].reshape(PATCH_NORTHWARD * PATCH_EASTWARD, OBS_TILE), measurement_noise_spread[batch_index].reshape(PATCH_NORTHWARD * PATCH_EASTWARD, OBS_TILE), active_measure_total[batch_index].reshape(PATCH_NORTHWARD * PATCH_EASTWARD), site_ids)
        packets_grid = packets.reshape(PATCH_NORTHWARD, PATCH_EASTWARD, MEMBER_TOTAL + 3, OBS_TILE)
        padded = jnp.pad(packets_grid, ((1, 1), (1, 1), (0, 0), (0, 0)))
        neighbours = jnp.stack([jnp.stack([padded[offset_row:offset_row + PATCH_NORTHWARD, offset_col:offset_col + PATCH_EASTWARD] for offset_col in range(3)], axis=2) for offset_row in range(3)], axis=2)
        neighbours = neighbours.reshape(PATCH_NORTHWARD * PATCH_EASTWARD, 3, 3, MEMBER_TOTAL + 3, OBS_TILE)
        member_fields = lax.map(lambda operands: tile_update(operands[0], unpack(operands[1])), (member_fields, neighbours))
    analysis = member_fields.reshape(PATCH_NORTHWARD, PATCH_EASTWARD, MEMBER_TOTAL, VERTICAL_LAYERS, PATCH_SPAN_NORTH, PATCH_SPAN_EAST)
    analysis = jnp.transpose(analysis, (2, 3, 0, 4, 1, 5)).reshape(MEMBER_TOTAL, VERTICAL_LAYERS, PATCH_NORTHWARD * PATCH_SPAN_NORTH, PATCH_EASTWARD * PATCH_SPAN_EAST)
    return analysis.astype(jnp.bfloat16)
```

```python
import functools

import jax
import jax.numpy as jnp
from jax import lax
from jax.experimental import pallas as pl
from jax.experimental.pallas import tpu as pltpu
from jax.sharding import PartitionSpec as P

MEMBERS = 64
LEVELS = 2
SPAN_NORTH = 4
SPAN_EAST = 512
SLOTS = 64
TILE_ROWS = 64
LINES = LEVELS * SPAN_NORTH
HALF = 256
PIECES = LINES * 2
STRIP = 128
STRIPS = SPAN_EAST // STRIP
REACH = 8
CHUNK = 64
SITE_CHUNK = 128
BATCH_LANES = 4 * SLOTS
F32 = jnp.float32
BF16 = jnp.bfloat16
VMEM_LIMIT = 48 * 1024 * 1024


def split(values):
    high = values.astype(BF16)
    return high, (values - high.astype(F32)).astype(BF16)


def relayout(wide, arranged, forward):
    for line in range(LINES):
        level, row = divmod(line, SPAN_NORTH)
        field_rows = pl.ds(level * TILE_ROWS * SPAN_NORTH + row, TILE_ROWS, stride=SPAN_NORTH)
        for strip in range(STRIPS):
            half, part = divmod(strip, 2)
            message_rows = pl.ds(2 * line + half, TILE_ROWS, stride=PIECES)
            if forward:
                arranged[part, message_rows, :] = wide[strip, field_rows, :]
            else:
                wide[strip, field_rows, :] = arranged[part, message_rows, :]


def pack_kernel(field_ref, message_ref, wide, arranged):
    for strip in range(STRIPS):
        wide[strip] = field_ref[:, strip * STRIP : (strip + 1) * STRIP].astype(F32)
    relayout(wide, arranged, True)
    for part in range(2):
        message_ref[:, part * STRIP : (part + 1) * STRIP] = arranged[part].astype(BF16)


def unpack_kernel(message_ref, field_ref, wide, arranged):
    for part in range(2):
        arranged[part] = message_ref[:, part * STRIP : (part + 1) * STRIP].astype(F32)
    relayout(wide, arranged, False)
    for strip in range(STRIPS):
        field_ref[:, strip * STRIP : (strip + 1) * STRIP] = wide[strip].astype(BF16)


def pick_kernel(field_ref, point_ref, raw_ref, scratch):
    point = point_ref[...]
    offset = point & (HALF - 1)
    piece = point >> 8
    place = lax.broadcasted_iota(jnp.int32, (HALF, 2 * SLOTS), 0)
    chooser = jnp.where(place == offset, 1.0, 0.0).astype(BF16)
    scratch[...] = jnp.dot(field_ref[...], chooser, preferred_element_type=F32)
    total = jnp.zeros((MEMBERS, 2 * SLOTS), F32)
    for index in range(PIECES):
        block = scratch[pl.ds(index, MEMBERS, stride=PIECES), :]
        total = total + jnp.where(piece == index, block, 0.0)
    raw_ref[...] = total.astype(BF16)


def weights_of(columns, datum, noise, live):
    mean = jnp.sum(columns, axis=0, keepdims=True) * (1.0 / MEMBERS)
    pert = columns - mean
    variance = jnp.sum(pert * pert, axis=0, keepdims=True) / (MEMBERS - 1)
    denominator = jnp.where(live > 0.0, variance + noise, 1.0)
    factor = 1.0 / (1.0 + jnp.sqrt(noise / denominator))
    return pert, live * (datum - mean) / denominator, live * factor / denominator


def positions(masks):
    rows, lanes = masks.shape
    before = lax.broadcasted_iota(jnp.int32, (128, 128), 0)
    after = lax.broadcasted_iota(jnp.int32, (128, 128), 1)
    triangle = jnp.where(before < after, 1.0, 0.0).astype(BF16)
    total = jnp.zeros((rows, 1), F32)
    parts = []
    for start in range(0, lanes, 128):
        block = masks[:, start : start + 128]
        rank = jnp.dot(block.astype(BF16), triangle, preferred_element_type=F32) + total
        parts.append(jnp.where(block > 0.0, rank, -1.0))
        total = total + jnp.sum(block, axis=1, keepdims=True)
    return jnp.concatenate(parts, axis=1), total


def taper(square):
    inverse = lax.rsqrt(jnp.maximum(square, 1.0))
    s = square * inverse * 0.25
    inside = (((-0.25 * s + 0.5) * s + 0.625) * s - 5.0 / 3.0) * s * s + 1.0
    outside = (
        ((((s * (1.0 / 12.0) - 0.5) * s + 0.625) * s + 5.0 / 3.0) * s - 5.0) * s
        + 4.0
        - (8.0 / 3.0) * inverse
    )
    return jnp.where(square <= 16.0, inside, jnp.where(square < 64.0, outside, 0.0))


def table_of(pert, mean_weight, pert_weight, row, col, level):
    high, low = split(pert)
    mean_high, mean_low = split(mean_weight)
    pert_high, pert_low = split(pert_weight)
    tail = [
        row.astype(F32).astype(BF16),
        (col & ~127).astype(F32).astype(BF16),
        (col & 127).astype(F32).astype(BF16),
        level.astype(F32).astype(BF16),
        mean_high,
        mean_low,
        pert_high,
        pert_low,
    ]
    lanes = pert.shape[1]
    rows = lax.broadcasted_iota(jnp.int32, (16, lanes), 0)
    block = jnp.zeros((16, lanes), F32)
    for index, line in enumerate(tail):
        block = jnp.where(rows == index, line.astype(F32), block)
    return high, low, block.astype(BF16)


def chosen_records(ranks, base, count, table):
    place = lax.broadcasted_iota(jnp.int32, (count, 1), 0).astype(F32) + base
    chooser = jnp.where(ranks == place, 1.0, 0.0).astype(BF16)
    return lax.dot_general(chooser, table, (((1,), (1,)), ((), ())), preferred_element_type=F32)


def open_records(records):
    pert = records[:, : 2 * MEMBERS].astype(BF16)
    tail = records[:, 2 * MEMBERS :]
    row = tail[:, 0:1]
    col = tail[:, 1:2] + tail[:, 2:3]
    level = tail[:, 3:4]
    mean_weight = tail[:, 4:5] + tail[:, 5:6]
    pert_weight = tail[:, 6:7] + tail[:, 7:8]
    step = mean_weight - pert_weight * (records[:, :MEMBERS] + records[:, MEMBERS : 2 * MEMBERS])
    high, low = split(step)
    return pert, row, col, level, jnp.concatenate([high, low, high], axis=0)


def advance(step, gain):
    high, low = split(gain)
    return lax.dot_general(
        step,
        jnp.concatenate([high, high, low], axis=0),
        (((0,), (0,)), ((), ())),
        preferred_element_type=F32,
    )


def level_factor(level, target):
    return (1.0 / (MEMBERS - 1)) / (1.0 + jnp.abs(level - float(target)))


def update_tile(ranks, total, table, source, state, wide_state):
    chunks = (jnp.max(total).astype(jnp.int32) + (CHUNK - 1)) // CHUNK

    def one(index, carry):
        base = (index * CHUNK).astype(F32)
        for strip in range(STRIPS):
            records = chosen_records(ranks[strip : strip + 1], base, CHUNK, table)
            pert, row, col, level, step = open_records(records)
            lane = lax.broadcasted_iota(jnp.int32, (1, STRIP), 1).astype(F32) + strip * STRIP
            across = col - lane
            across = across * across
            tapers = []
            for line in range(SPAN_NORTH):
                down = row - float(line)
                tapers.append(taper(across + down * down))
            weight = jnp.concatenate(
                [t * level_factor(level, target) for target in range(LEVELS) for t in tapers], axis=1
            )
            if wide_state:
                pert = jnp.concatenate([pert, pert[:, :MEMBERS]], axis=1)
            covariance = jnp.dot(pert, source[strip], preferred_element_type=F32)
            state[strip] = state[strip] + advance(step, weight * covariance)
        return carry

    lax.fori_loop(0, chunks, one, 0)


def analysis_kernel(
    field_ref, cat_n2, cat_n1, cat_0, cat_s1, cat_s2, meta_n2, meta_n1, meta_0, meta_s1, meta_s2,
    message_ref, wide, state, narrow, source, site_state,
):
    for part in range(2):
        wide[part] = field_ref[:, part * STRIP : (part + 1) * STRIP].astype(F32)
    for strip in range(STRIPS):
        half, part = divmod(strip, 2)
        for line in range(LINES):
            piece = wide[part, pl.ds(2 * line + half, MEMBERS, stride=PIECES), :]
            lanes = pl.ds(line * STRIP, STRIP)
            state[strip, :, lanes] = piece
            low = piece.astype(BF16)
            narrow[strip, :MEMBERS, lanes] = low
            narrow[strip, MEMBERS:, lanes] = low

    def facts(metas, rows, batch):
        lanes = pl.ds(batch * BATCH_LANES, BATCH_LANES)
        meta = jnp.concatenate([m[:, lanes] for m in metas], axis=1)
        point = meta[2:3].astype(jnp.int32)
        lane = lax.broadcasted_iota(jnp.int32, point.shape, 1)
        tile_row = (lane >> 8) - rows
        tile_col = ((lane >> 6) & 3) - 1
        row = tile_row * SPAN_NORTH + ((point >> 9) & 3)
        col = tile_col * SPAN_EAST + (point & (SPAN_EAST - 1))
        return meta[0:1], meta[1:2], meta[3:4], row, col, point >> 11

    def strip_masks(col, live):
        rows = lax.broadcasted_iota(jnp.int32, (8, col.shape[1]), 0)
        west = rows * STRIP - REACH
        inside = (col > west) & (col < west + STRIP + 2 * REACH - 1) & (rows < STRIPS)
        return jnp.where(inside, live, 0.0)

    first = jnp.concatenate(
        [c[:, pl.ds(0, BATCH_LANES)] for c in (cat_n2, cat_n1, cat_0, cat_s1, cat_s2)], axis=1
    ).astype(F32)
    datum, noise, live, row, col, level = facts((meta_n2, meta_n1, meta_0, meta_s1, meta_s2), 2, 0)
    pert, mean_weight, pert_weight = weights_of(first, datum, noise, live)
    table = jnp.concatenate(
        table_of(pert, mean_weight, pert_weight, row, col, level), axis=0
    )
    near = slice(BATCH_LANES, 4 * BATCH_LANES)
    ranks, total = positions(strip_masks(col[:, near], live[:, near]))
    update_tile(ranks, total, table[:, near], narrow, state, False)

    sites = jnp.concatenate(
        [c[:, pl.ds(BATCH_LANES, BATCH_LANES)] for c in (cat_n1, cat_0, cat_s1)], axis=1
    )
    site_state[...] = sites.astype(F32)
    datum_1, noise_1, live_1, row_1, col_1, level_1 = facts((meta_n1, meta_0, meta_s1), 1, 1)
    reached = (col > -2 * REACH) & (col < SPAN_EAST + 2 * REACH - 1)
    wanted = jnp.broadcast_to(jnp.where(reached, live, 0.0), (8, col.shape[1]))
    site_ranks, site_total = positions(wanted)
    site_row = row_1.astype(F32)
    site_col = col_1.astype(F32)
    site_level = level_1.astype(F32)
    site_tile = (row_1 >> 2).astype(F32)
    doubled = jnp.concatenate([sites, sites], axis=0)

    def one(index, carry):
        base = (index * SITE_CHUNK).astype(F32)
        records = chosen_records(site_ranks[0:1], base, SITE_CHUNK, table)
        obs, obs_row, obs_col, obs_level, step = open_records(records)
        down = obs_row - site_row
        across = obs_col - site_col
        weight = taper(down * down + across * across)
        weight = weight * ((1.0 / (MEMBERS - 1)) / (1.0 + jnp.abs(obs_level - site_level)))
        obs_tile = jnp.floor(obs_row * (1.0 / SPAN_NORTH))
        weight = jnp.where(jnp.abs(obs_tile - site_tile) <= 1.0, weight, 0.0)
        covariance = jnp.dot(obs, doubled, preferred_element_type=F32)
        site_state[...] = site_state[...] + advance(step, weight * covariance)
        return carry

    chunks = (jnp.max(site_total).astype(jnp.int32) + (SITE_CHUNK - 1)) // SITE_CHUNK
    lax.fori_loop(0, chunks, one, 0)

    pert, mean_weight, pert_weight = weights_of(site_state[...], datum_1, noise_1, live_1)
    table_1 = jnp.concatenate(
        table_of(pert, mean_weight, pert_weight, row_1, col_1, level_1), axis=0
    )
    ranks_1, total_1 = positions(strip_masks(col_1, live_1))
    for strip in range(STRIPS):
        high, low = split(state[strip])
        source[strip, :MEMBERS, :] = high
        source[strip, MEMBERS : 2 * MEMBERS, :] = high
        source[strip, 2 * MEMBERS :, :] = low
    update_tile(ranks_1, total_1, table_1, source, state, True)

    for strip in range(STRIPS):
        half, part = divmod(strip, 2)
        for line in range(LINES):
            wide[part, pl.ds(2 * line + half, MEMBERS, stride=PIECES), :] = state[
                strip, :, pl.ds(line * STRIP, STRIP)
            ]
    for part in range(2):
        message_ref[:, part * STRIP : (part + 1) * STRIP] = wide[part].astype(BF16)


def pack(field):
    return pl.pallas_call(
        pack_kernel,
        out_shape=jax.ShapeDtypeStruct((TILE_ROWS * PIECES, HALF), BF16),
        scratch_shapes=[
            pltpu.VMEM((STRIPS, LEVELS * TILE_ROWS * SPAN_NORTH, STRIP), F32),
            pltpu.VMEM((2, TILE_ROWS * PIECES, STRIP), F32),
        ],
        compiler_params=pltpu.CompilerParams(vmem_limit_bytes=VMEM_LIMIT),
        cost_estimate=pl.CostEstimate(flops=0, bytes_accessed=1 << 20, transcendentals=0),
    )(field)


def unpack(message):
    return pl.pallas_call(
        unpack_kernel,
        out_shape=jax.ShapeDtypeStruct((LEVELS * TILE_ROWS * SPAN_NORTH, SPAN_EAST), BF16),
        scratch_shapes=[
            pltpu.VMEM((STRIPS, LEVELS * TILE_ROWS * SPAN_NORTH, STRIP), F32),
            pltpu.VMEM((2, TILE_ROWS * PIECES, STRIP), F32),
        ],
        compiler_params=pltpu.CompilerParams(vmem_limit_bytes=VMEM_LIMIT),
        cost_estimate=pl.CostEstimate(flops=0, bytes_accessed=1 << 20, transcendentals=0),
    )(message)


def pick(field, points):
    return pl.pallas_call(
        pick_kernel,
        out_shape=jax.ShapeDtypeStruct((MEMBERS, 2 * SLOTS), BF16),
        scratch_shapes=[pltpu.VMEM((MEMBERS * PIECES, 2 * SLOTS), F32)],
        compiler_params=pltpu.CompilerParams(vmem_limit_bytes=VMEM_LIMIT),
        cost_estimate=pl.CostEstimate(flops=1 << 26, bytes_accessed=1 << 19, transcendentals=0),
    )(field, points)


def analyse(field, cats, metas):
    return pl.pallas_call(
        analysis_kernel,
        out_shape=jax.ShapeDtypeStruct((MEMBERS * PIECES, HALF), BF16),
        scratch_shapes=[
            pltpu.VMEM((2, MEMBERS * PIECES, STRIP), F32),
            pltpu.VMEM((STRIPS, MEMBERS, LINES * STRIP), F32),
            pltpu.VMEM((STRIPS, 2 * MEMBERS, LINES * STRIP), BF16),
            pltpu.VMEM((STRIPS, 3 * MEMBERS, LINES * STRIP), BF16),
            pltpu.VMEM((MEMBERS, 3 * BATCH_LANES), F32),
        ],
        compiler_params=pltpu.CompilerParams(vmem_limit_bytes=VMEM_LIMIT),
        cost_estimate=pl.CostEstimate(flops=1 << 30, bytes_accessed=1 << 20, transcendentals=0),
    )(field, *cats, *metas)


def from_behind(block, axis, distance):
    size = lax.axis_size(axis)
    route = [(i - distance, i) for i in range(size) if 0 <= i - distance < size]
    return lax.ppermute(block, axis, route)


def gather_row(own):
    west = from_behind(own, "tile", 1)
    east = from_behind(own, "tile", -1)
    none = jnp.zeros((own.shape[0], SLOTS), own.dtype)
    parts = []
    for batch in range(2):
        lanes = slice(batch * SLOTS, (batch + 1) * SLOTS)
        parts += [west[:, lanes], own[:, lanes], east[:, lanes], none]
    return jnp.concatenate(parts, axis=1)


def gather_column(row):
    first = row[:, :BATCH_LANES]
    return (
        from_behind(first, "mem", 2),
        from_behind(row, "mem", 1),
        row,
        from_behind(row, "mem", -1),
        from_behind(first, "mem", -2),
    )


def on_device(members, datum, noise, point, count):
    message = pack(members.reshape(LEVELS * TILE_ROWS * SPAN_NORTH, SPAN_EAST))
    field = lax.all_to_all(message, "mem", split_axis=0, concat_axis=0, tiled=True)

    point = point.reshape(1, 2 * SLOTS)
    slot = lax.broadcasted_iota(jnp.int32, (2, SLOTS), 1)
    live = (slot < count.reshape(2, 1)).astype(F32).reshape(1, 2 * SLOTS)
    meta = jnp.concatenate(
        [
            datum.reshape(1, 2 * SLOTS),
            noise.reshape(1, 2 * SLOTS),
            point.astype(F32),
            live,
            jnp.zeros((4, 2 * SLOTS), F32),
        ],
        axis=0,
    )
    metas = gather_column(gather_row(meta))
    cats = gather_column(gather_row(pick(field, point)))
    returned = analyse(field, cats, metas)
    message = lax.all_to_all(returned, "mem", split_axis=0, concat_axis=0, tiled=True)
    return unpack(message).reshape(1, LEVELS, TILE_ROWS * SPAN_NORTH, SPAN_EAST)


def solution(mesh):
    return jax.shard_map(
        on_device,
        mesh=mesh,
        in_specs=(
            P("mem", None, None, "tile"),
            P(None, "mem", "tile", None),
            P(None, "mem", "tile", None),
            P(None, "mem", "tile", None),
            P(None, "mem", "tile"),
        ),
        out_specs=P("mem", None, None, "tile"),
        check_vma=False,
    )
```

```python
import jax
import jax.numpy as jnp
from jax import lax
from jax.experimental import pallas as pl
from jax.experimental.pallas import tpu as pltpu
from jax.sharding import PartitionSpec as P

MEMBERS = 64
LEVELS = 2
SPAN_NORTH = 4
SPAN_EAST = 512
SLOTS = 64
CHIPS = 32
ROWS = 2 * SPAN_NORTH
LINES = LEVELS * ROWS
HALF = SPAN_EAST // 2
STRIP = 128
STRIPS = HALF // STRIP
REACH = 8
CHUNK = 64
SITE_CHUNK = 128
FACTS = 16
PACKET = MEMBERS + FACTS
BATCH_LANES = 4 * SLOTS
F32 = jnp.float32
BF16 = jnp.bfloat16
VMEM_LIMIT = 48 * 1024 * 1024


def split(values):
    high = values.astype(BF16)
    return high, (values - high.astype(F32)).astype(BF16)


def pack_kernel(field_ref, message_ref):
    for group in range(CHIPS // 2):
        upper, lower = (
            field_ref[level, pl.ds(2 * ROWS * group, 2 * ROWS), :].astype(F32) for level in range(LEVELS)
        )
        for chip in range(2):
            rows = slice(chip * ROWS, (chip + 1) * ROWS)
            for half in range(2):
                lanes = slice(half * HALF, (half + 1) * HALF)
                place = (2 * (2 * group + chip) + half) * LINES
                message_ref[pl.ds(place, LINES), :] = jnp.concatenate(
                    [upper[rows, lanes], lower[rows, lanes]], axis=0
                ).astype(BF16)


def unpack_kernel(message_ref, field_ref):
    for group in range(CHIPS // 2):
        for half in range(2):
            lanes = pl.ds(half * HALF, HALF)
            first, second = (
                message_ref[pl.ds((2 * (2 * group + chip) + half) * LINES, LINES), :].astype(F32)
                for chip in range(2)
            )
            for level in range(LEVELS):
                rows = slice(level * ROWS, (level + 1) * ROWS)
                field_ref[level, pl.ds(2 * ROWS * group, 2 * ROWS), lanes] = jnp.concatenate(
                    [first[rows], second[rows]], axis=0
                ).astype(BF16)


def parts_of(values):
    high = values.astype(BF16).astype(F32)
    rest = values - high
    middle = rest.astype(BF16).astype(F32)
    return [high, middle, rest - middle]


def stack_rows(lines, count):
    shape = (count, lines[0].shape[1])
    rows = lax.broadcasted_iota(jnp.int32, shape, 0)
    block = jnp.zeros(shape, F32)
    for index, line in enumerate(lines):
        block = jnp.where(rows == index, line, block)
    return block


def facts_kernel(place_ref, datum_ref, noise_ref, point_ref, count_ref, facts_ref):
    lane = lax.broadcasted_iota(jnp.int32, (1, 2 * SLOTS), 1)

    def both(ref):
        first = jnp.concatenate([ref[0, 0], ref[0, 0]], axis=1)
        second = jnp.concatenate([ref[1, 0], ref[1, 0]], axis=1)
        return jnp.where(lane < SLOTS, first, second)

    point = both(point_ref)
    count = jnp.where(lane < SLOTS, count_ref[0], count_ref[1])
    col = place_ref[1] + (point & (SPAN_EAST - 1))
    row = place_ref[0] + ((point >> 9) & (SPAN_NORTH - 1))
    live = jnp.where((lane & (SLOTS - 1)) < count, 1.0, 0.0)
    lines = parts_of(both(datum_ref)) + parts_of(both(noise_ref))
    lines += [(col >> 7).astype(F32), (col & 127).astype(F32), row.astype(F32), (point >> 11).astype(F32), live]
    facts_ref[...] = stack_rows(lines, FACTS).astype(BF16)


def pick_kernel(place_ref, field_ref, own_ref, other_ref, packet_ref, scratch):
    own = own_ref[...].astype(F32)
    other = other_ref[...].astype(F32)
    half = place_ref[2]
    first = jnp.where(half == 0, own, other)
    second = jnp.where(half == 0, other, own)
    lane = lax.broadcasted_iota(jnp.int32, first.shape, 1)
    batches = (
        jnp.where(lane < SLOTS, first, pltpu.roll(second, SLOTS, 1)),
        jnp.where(lane < SLOTS, pltpu.roll(first, SLOTS, 1), second),
    )
    place = lax.broadcasted_iota(jnp.int32, (HALF, 2 * SLOTS), 0)
    for batch in range(2):
        facts = batches[batch]
        col = (facts[6:7] * 128.0 + facts[7:8]).astype(jnp.int32) - place_ref[4]
        line = (facts[9:10] * ROWS + facts[8:9]).astype(jnp.int32) - place_ref[3]
        chooser = jnp.where(place == col, 1.0, 0.0).astype(BF16)
        scratch[...] = jnp.dot(field_ref[...], chooser, preferred_element_type=F32)
        total = jnp.zeros((MEMBERS, 2 * SLOTS), F32)
        for index in range(LINES):
            block = scratch[pl.ds(index, MEMBERS, stride=LINES), :]
            total = total + jnp.where(line == index, block, 0.0)
        lanes = pl.ds(batch * 2 * SLOTS, 2 * SLOTS)
        packet_ref[pl.ds(0, MEMBERS), lanes] = total.astype(BF16)
        packet_ref[pl.ds(MEMBERS, FACTS), lanes] = facts.astype(BF16)


def merge_kernel(own_ref, other_ref, beyond_ref, cat_ref):
    for batch in range(2):
        lanes = pl.ds(batch * 2 * SLOTS, 2 * SLOTS)
        here = pl.ds(batch * BATCH_LANES, 2 * SLOTS)
        members = pl.ds(0, MEMBERS)
        facts = pl.ds(MEMBERS, FACTS)
        cat_ref[members, here] = own_ref[members, lanes] + other_ref[members, lanes]
        cat_ref[facts, here] = own_ref[facts, lanes]
        cat_ref[:, pl.ds(batch * BATCH_LANES + 2 * SLOTS, 2 * SLOTS)] = beyond_ref[:, lanes]


def weights_of(columns, datum, noise, live):
    mean = jnp.sum(columns, axis=0, keepdims=True) * (1.0 / MEMBERS)
    pert = columns - mean
    variance = jnp.sum(pert * pert, axis=0, keepdims=True) / (MEMBERS - 1)
    denominator = jnp.where(live > 0.0, variance + noise, 1.0)
    factor = 1.0 / (1.0 + jnp.sqrt(noise / denominator))
    return pert, live * (datum - mean) / denominator, live * factor / denominator


def positions(masks):
    rows, lanes = masks.shape
    before = lax.broadcasted_iota(jnp.int32, (128, 128), 0)
    after = lax.broadcasted_iota(jnp.int32, (128, 128), 1)
    triangle = jnp.where(before < after, 1.0, 0.0).astype(BF16)
    total = jnp.zeros((rows, 1), F32)
    parts = []
    for start in range(0, lanes, 128):
        block = masks[:, start : start + 128]
        rank = jnp.dot(block.astype(BF16), triangle, preferred_element_type=F32) + total
        parts.append(jnp.where(block > 0.0, rank, -1.0))
        total = total + jnp.sum(block, axis=1, keepdims=True)
    return jnp.concatenate(parts, axis=1), total


def taper(square):
    inverse = lax.rsqrt(jnp.maximum(square, 1.0))
    s = square * inverse * 0.25
    inside = (((-0.25 * s + 0.5) * s + 0.625) * s - 5.0 / 3.0) * s * s + 1.0
    outside = (
        ((((s * (1.0 / 12.0) - 0.5) * s + 0.625) * s + 5.0 / 3.0) * s - 5.0) * s
        + 4.0
        - (8.0 / 3.0) * inverse
    )
    return jnp.where(square <= 16.0, inside, jnp.where(square < 64.0, outside, 0.0))


def table_of(pert, mean_weight, pert_weight, row, col, level):
    high, low = split(pert)
    tail = [row.astype(F32), (col & ~127).astype(F32), (col & 127).astype(F32), level]
    for weight in (mean_weight, pert_weight):
        weight_high, weight_low = split(weight)
        tail += [weight_high.astype(F32), weight_low.astype(F32)]
    return jnp.concatenate([high, low, stack_rows(tail, 16).astype(BF16)], axis=0)


def chosen_records(ranks, base, count, table):
    place = lax.broadcasted_iota(jnp.int32, (count, 1), 0).astype(F32) + base
    chooser = jnp.where(ranks == place, 1.0, 0.0).astype(BF16)
    return lax.dot_general(chooser, table, (((1,), (1,)), ((), ())), preferred_element_type=F32)


def open_records(records):
    pert = records[:, : 2 * MEMBERS].astype(BF16)
    tail = records[:, 2 * MEMBERS :]
    row = tail[:, 0:1]
    col = tail[:, 1:2] + tail[:, 2:3]
    level = tail[:, 3:4]
    mean_weight = tail[:, 4:5] + tail[:, 5:6]
    pert_weight = tail[:, 6:7] + tail[:, 7:8]
    step = mean_weight - pert_weight * (records[:, :MEMBERS] + records[:, MEMBERS : 2 * MEMBERS])
    high, low = split(step)
    return pert, row, col, level, jnp.concatenate([high, low, high], axis=0)


def advance(step, gain):
    high, low = split(gain)
    return lax.dot_general(
        step,
        jnp.concatenate([high, high, low], axis=0),
        (((0,), (0,)), ((), ())),
        preferred_element_type=F32,
    )


def level_factor(level, target):
    return (1.0 / (MEMBERS - 1)) / (1.0 + jnp.abs(level - target))


def update_region(ranks, total, table, source, state, wide_state):
    chunks = (jnp.max(total).astype(jnp.int32) + (CHUNK - 1)) // CHUNK

    def one(index, carry):
        base = (index * CHUNK).astype(F32)
        for strip in range(STRIPS):
            records = chosen_records(ranks[strip : strip + 1], base, CHUNK, table)
            pert, row, col, level, step = open_records(records)
            lane = lax.broadcasted_iota(jnp.int32, (1, STRIP), 1).astype(F32) + strip * STRIP
            across = col - lane
            across = across * across
            tile = jnp.floor(row * (1.0 / SPAN_NORTH))
            beside = [
                jnp.where(jnp.abs(tile - target) <= 1.0, 1.0, 0.0) for target in range(ROWS // SPAN_NORTH)
            ]
            tapers = []
            for line in range(ROWS):
                down = row - float(line)
                tapers.append(taper(across + down * down) * beside[line // SPAN_NORTH])
            if wide_state:
                pert = jnp.concatenate([pert, pert[:, :MEMBERS]], axis=1)
            for target in range(LEVELS):
                lanes = pl.ds(target * ROWS * STRIP, ROWS * STRIP)
                factor = level_factor(level, float(target))
                weight = jnp.concatenate([t * factor for t in tapers], axis=1)
                covariance = jnp.dot(pert, source[strip, :, lanes], preferred_element_type=F32)
                state[strip, :, lanes] = state[strip, :, lanes] + advance(step, weight * covariance)
        return carry

    lax.fori_loop(0, chunks, one, 0)


def facts_of(cats, batch, place_ref):
    lanes = pl.ds(batch * BATCH_LANES, BATCH_LANES)
    facts = jnp.concatenate([c[pl.ds(MEMBERS, FACTS), lanes] for c in cats], axis=1).astype(F32)
    datum = facts[0:1] + facts[1:2] + facts[2:3]
    noise = facts[3:4] + facts[4:5] + facts[5:6]
    col = (facts[6:7] * 128.0 + facts[7:8]).astype(jnp.int32) - place_ref[4]
    row = facts[8:9].astype(jnp.int32) - place_ref[3]
    return datum, noise, col, row, facts[9:10], facts[10:11]


def masks_of(col, row, live):
    masks = []
    for strip in range(STRIPS):
        west = strip * STRIP - REACH
        inside = (col > west) & (col < west + STRIP + 2 * REACH - 1)
        inside = inside & (row >= -SPAN_NORTH) & (row < ROWS + SPAN_NORTH)
        masks.append(jnp.where(inside, live, 0.0))
    inside = (col > -2 * REACH) & (col < HALF + 2 * REACH - 1)
    masks.append(jnp.where(inside, live, 0.0))
    return stack_rows(masks, 8)


def analysis_kernel(
    place_ref, field_ref, north_ref, here_ref, south_ref, message_ref, wide, state, narrow, source, site_state
):
    cats = (north_ref, here_ref, south_ref)
    for part in range(STRIPS):
        wide[part] = field_ref[:, part * STRIP : (part + 1) * STRIP].astype(F32)
    for strip in range(STRIPS):
        for line in range(LINES):
            piece = wide[strip, pl.ds(line, MEMBERS, stride=LINES), :]
            lanes = pl.ds(line * STRIP, STRIP)
            state[strip, :, lanes] = piece
            low = piece.astype(BF16)
            narrow[strip, :MEMBERS, lanes] = low
            narrow[strip, MEMBERS:, lanes] = low

    first, sites = (
        jnp.concatenate([c[pl.ds(0, MEMBERS), pl.ds(b * BATCH_LANES, BATCH_LANES)] for c in cats], axis=1)
        for b in range(2)
    )
    datum, noise, col, row, level, live = facts_of(cats, 0, place_ref)
    pert, mean_weight, pert_weight = weights_of(first.astype(F32), datum, noise, live)
    table = table_of(pert, mean_weight, pert_weight, row, col, level)
    ranks, total = positions(masks_of(col, row, live))
    update_region(ranks, total[:STRIPS], table, narrow, state, False)

    site_state[...] = sites.astype(F32)
    datum_1, noise_1, col_1, row_1, level_1, live_1 = facts_of(cats, 1, place_ref)
    site_row = row_1.astype(F32)
    site_col = col_1.astype(F32)
    site_tile = (row_1 >> 2).astype(F32)
    doubled = jnp.concatenate([sites, sites], axis=0)

    def one(index, carry):
        base = (index * SITE_CHUNK).astype(F32)
        records = chosen_records(ranks[STRIPS : STRIPS + 1], base, SITE_CHUNK, table)
        obs, obs_row, obs_col, obs_level, step = open_records(records)
        down = obs_row - site_row
        across = obs_col - site_col
        weight = taper(down * down + across * across) * level_factor(obs_level, level_1)
        obs_tile = jnp.floor(obs_row * (1.0 / SPAN_NORTH))
        weight = jnp.where(jnp.abs(obs_tile - site_tile) <= 1.0, weight, 0.0)
        covariance = jnp.dot(obs, doubled, preferred_element_type=F32)
        site_state[...] = site_state[...] + advance(step, weight * covariance)
        return carry

    chunks = (jnp.max(total[STRIPS : STRIPS + 1]).astype(jnp.int32) + (SITE_CHUNK - 1)) // SITE_CHUNK
    lax.fori_loop(0, chunks, one, 0)

    pert, mean_weight, pert_weight = weights_of(site_state[...], datum_1, noise_1, live_1)
    table_1 = table_of(pert, mean_weight, pert_weight, row_1, col_1, level_1)
    ranks_1, total_1 = positions(masks_of(col_1, row_1, live_1))
    for strip in range(STRIPS):
        high, low = split(state[strip])
        source[strip, :MEMBERS, :] = high
        source[strip, MEMBERS : 2 * MEMBERS, :] = high
        source[strip, 2 * MEMBERS :, :] = low
    update_region(ranks_1, total_1[:STRIPS], table_1, source, state, True)

    for strip in range(STRIPS):
        for line in range(LINES):
            wide[strip, pl.ds(line, MEMBERS, stride=LINES), :] = state[strip, :, pl.ds(line * STRIP, STRIP)]
    for part in range(STRIPS):
        message_ref[:, part * STRIP : (part + 1) * STRIP] = wide[part].astype(BF16)


def call(kernel, shape, operands, scratch=(), scalars=0, flops=0, moved=1 << 18):
    smem = pl.BlockSpec(memory_space=pltpu.SMEM)
    vmem = pl.BlockSpec(memory_space=pltpu.VMEM)
    return pl.pallas_call(
        kernel,
        out_shape=jax.ShapeDtypeStruct(shape, BF16),
        in_specs=[smem if index < scalars else vmem for index in range(len(operands))],
        out_specs=vmem,
        scratch_shapes=list(scratch),
        compiler_params=pltpu.CompilerParams(vmem_limit_bytes=VMEM_LIMIT),
        cost_estimate=pl.CostEstimate(flops=flops, bytes_accessed=moved, transcendentals=0),
    )(*operands)


MESSAGE = (MEMBERS * LINES, HALF)


def pack(field):
    return call(pack_kernel, MESSAGE, (field,), moved=1 << 20)


def unpack(message):
    return call(unpack_kernel, (LEVELS, CHIPS * ROWS, SPAN_EAST), (message,), moved=1 << 20)


def state_facts(place, datum, noise, point, count):
    smem = pl.BlockSpec(memory_space=pltpu.SMEM)
    vmem = pl.BlockSpec(memory_space=pltpu.VMEM)
    return pl.pallas_call(
        facts_kernel,
        out_shape=jax.ShapeDtypeStruct((FACTS, 2 * SLOTS), BF16),
        in_specs=[smem, vmem, vmem, vmem, smem],
        out_specs=vmem,
        compiler_params=pltpu.CompilerParams(vmem_limit_bytes=VMEM_LIMIT),
    )(place, datum, noise, point, count)


def pick(place, field, own, other):
    scratch = [pltpu.VMEM((MEMBERS * LINES, 2 * SLOTS), F32)]
    return call(
        pick_kernel, (PACKET, 4 * SLOTS), (place, field, own, other), scratch, 1, 1 << 27, 1 << 19
    )


def merge(own, other, beyond):
    return call(merge_kernel, (PACKET, 2 * BATCH_LANES), (own, other, beyond))


def analyse(place, field, north, here, south):
    scratch = [
        pltpu.VMEM((STRIPS, MEMBERS * LINES, STRIP), F32),
        pltpu.VMEM((STRIPS, MEMBERS, LINES * STRIP), F32),
        pltpu.VMEM((STRIPS, 2 * MEMBERS, LINES * STRIP), BF16),
        pltpu.VMEM((STRIPS, 3 * MEMBERS, LINES * STRIP), BF16),
        pltpu.VMEM((MEMBERS, 3 * BATCH_LANES), F32),
    ]
    return call(
        analysis_kernel, MESSAGE, (place, field, north, here, south), scratch, 1, 1 << 30, 1 << 20
    )


def swap_cores(block):
    return lax.ppermute(block, "mem", [(i, i ^ 1) for i in range(lax.axis_size("mem"))])


def swap_beyond(block):
    rows, columns = lax.axis_size("mem"), lax.axis_size("tile")
    route = []
    for row in range(0, rows, 2):
        for column in range(columns - 1):
            west, east = (row + 1) * columns + column, row * columns + column + 1
            route += [(west, east), (east, west)]
    return lax.ppermute(block, ("mem", "tile"), route)


def from_behind(block, distance):
    size = lax.axis_size("mem")
    route = [(i - distance, i) for i in range(size) if 0 <= i - distance < size]
    return lax.ppermute(block, "mem", route)


def on_device(members, datum, noise, point, count):
    row = lax.axis_index("mem")
    column = lax.axis_index("tile")
    half = row % 2
    place = jnp.stack(
        [row * SPAN_NORTH, column * SPAN_EAST, half, (row // 2) * ROWS, column * SPAN_EAST + half * HALF]
    ).astype(jnp.int32)
    message = pack(members[0])
    field = lax.all_to_all(message, "mem", split_axis=0, concat_axis=0, tiled=True)
    facts = state_facts(place, datum, noise, point, count.reshape(2))
    packet = pick(place, field, facts, swap_cores(facts))
    here = merge(packet, swap_cores(packet), swap_beyond(packet))
    north, south = from_behind(here, 2), from_behind(here, -2)
    message = analyse(place, field, north, here, south)
    message = lax.all_to_all(message, "mem", split_axis=0, concat_axis=0, tiled=True)
    return unpack(message)[None]


def solution(mesh):
    return jax.shard_map(
        on_device,
        mesh=mesh,
        in_specs=(
            P("mem", None, None, "tile"),
            P(None, "mem", "tile", None),
            P(None, "mem", "tile", None),
            P(None, "mem", "tile", None),
            P(None, "mem", "tile"),
        ),
        out_specs=P("mem", None, None, "tile"),
        check_vma=False,
    )
```

```python
import functools

import jax
import jax.numpy as jnp
from jax import lax
from jax.experimental import pallas as pl
from jax.experimental.pallas import tpu as pltpu
from jax.sharding import PartitionSpec as P

MEMBERS = 64
LEVELS = 2
SPAN_NORTH = 4
SPAN_EAST = 512
SLOTS = 64
CHIPS = 32
ROWS = 2 * SPAN_NORTH
LINES = LEVELS * ROWS
HALF = SPAN_EAST // 2
STRIP = 128
STRIPS = HALF // STRIP
REACH = 8
CHUNK = 64
SITE_CHUNK = 160
FACTS = 16
PACKET = MEMBERS + FACTS
BATCH_LANES = 4 * SLOTS
F32 = jnp.float32
BF16 = jnp.bfloat16
VMEM_LIMIT = 48 * 1024 * 1024


def split(values):
    high = values.astype(BF16)
    return high, (values - high.astype(F32)).astype(BF16)


def pack_kernel(field_ref, message_ref):
    for group in range(CHIPS // 2):
        upper, lower = (
            field_ref[level, pl.ds(2 * ROWS * group, 2 * ROWS), :].astype(F32) for level in range(LEVELS)
        )
        for chip in range(2):
            rows = slice(chip * ROWS, (chip + 1) * ROWS)
            for half in range(2):
                lanes = slice(half * HALF, (half + 1) * HALF)
                place = (2 * (2 * group + chip) + half) * LINES
                message_ref[pl.ds(place, LINES), :] = jnp.concatenate(
                    [upper[rows, lanes], lower[rows, lanes]], axis=0
                ).astype(BF16)


def unpack_kernel(message_ref, field_ref):
    for group in range(CHIPS // 2):
        for half in range(2):
            lanes = pl.ds(half * HALF, HALF)
            first, second = (
                message_ref[pl.ds((2 * (2 * group + chip) + half) * LINES, LINES), :].astype(F32)
                for chip in range(2)
            )
            for level in range(LEVELS):
                rows = slice(level * ROWS, (level + 1) * ROWS)
                field_ref[level, pl.ds(2 * ROWS * group, 2 * ROWS), lanes] = jnp.concatenate(
                    [first[rows], second[rows]], axis=0
                ).astype(BF16)


def parts_of(values):
    high = values.astype(BF16).astype(F32)
    rest = values - high
    middle = rest.astype(BF16).astype(F32)
    return [high, middle, rest - middle]


def stack_rows(lines, count):
    shape = (count, lines[0].shape[1])
    rows = lax.broadcasted_iota(jnp.int32, shape, 0)
    block = jnp.zeros(shape, F32)
    for index, line in enumerate(lines):
        block = jnp.where(rows == index, line, block)
    return block


def facts_kernel(place_ref, datum_ref, noise_ref, point_ref, count_ref, facts_ref):
    lane = lax.broadcasted_iota(jnp.int32, (1, 2 * SLOTS), 1)

    def both(ref):
        first = jnp.concatenate([ref[0, 0], ref[0, 0]], axis=1)
        second = jnp.concatenate([ref[1, 0], ref[1, 0]], axis=1)
        return jnp.where(lane < SLOTS, first, second)

    point = both(point_ref)
    count = jnp.where(lane < SLOTS, count_ref[0], count_ref[1])
    col = place_ref[1] + (point & (SPAN_EAST - 1))
    row = place_ref[0] + ((point >> 9) & (SPAN_NORTH - 1))
    live = jnp.where((lane & (SLOTS - 1)) < count, 1.0, 0.0)
    lines = parts_of(both(datum_ref)) + parts_of(both(noise_ref))
    lines += [(col >> 7).astype(F32), (col & 127).astype(F32), row.astype(F32), (point >> 11).astype(F32), live]
    facts_ref[...] = stack_rows(lines, FACTS).astype(BF16)


def pick_kernel(place_ref, field_ref, own_ref, other_ref, packet_ref, scratch):
    own = own_ref[...].astype(F32)
    other = other_ref[...].astype(F32)
    half = place_ref[2]
    first = jnp.where(half == 0, own, other)
    second = jnp.where(half == 0, other, own)
    lane = lax.broadcasted_iota(jnp.int32, first.shape, 1)
    batches = (
        jnp.where(lane < SLOTS, first, pltpu.roll(second, SLOTS, 1)),
        jnp.where(lane < SLOTS, pltpu.roll(first, SLOTS, 1), second),
    )
    place = lax.broadcasted_iota(jnp.int32, (HALF, 2 * SLOTS), 0)
    choosers, lines = [], []
    for facts in batches:
        col = (facts[6:7] * 128.0 + facts[7:8]).astype(jnp.int32) - place_ref[4]
        lines.append((facts[9:10] * ROWS + facts[8:9]).astype(jnp.int32) - place_ref[3])
        choosers.append(jnp.where(place == col, 1.0, 0.0).astype(BF16))
    values = jnp.dot(field_ref[...], jnp.concatenate(choosers, axis=1), preferred_element_type=F32)
    for batch in range(2):
        lanes = pl.ds(batch * 2 * SLOTS, 2 * SLOTS)
        scratch[batch] = values[:, batch * 2 * SLOTS : (batch + 1) * 2 * SLOTS]
        total = jnp.zeros((MEMBERS, 2 * SLOTS), F32)
        for index in range(LINES):
            block = scratch[batch, pl.ds(index, MEMBERS, stride=LINES), :]
            total = total + jnp.where(lines[batch] == index, block, 0.0)
        packet_ref[pl.ds(0, MEMBERS), lanes] = total.astype(BF16)
        packet_ref[pl.ds(MEMBERS, FACTS), lanes] = batches[batch].astype(BF16)


def merge_kernel(own_ref, other_ref, beyond_ref, cat_ref):
    lane = lax.broadcasted_iota(jnp.int32, (PACKET, 2 * SLOTS), 1)
    for batch in range(2):
        lanes = pl.ds(batch * 2 * SLOTS, 2 * SLOTS)
        members = pl.ds(0, MEMBERS)
        here = jnp.concatenate(
            [own_ref[members, lanes] + other_ref[members, lanes], own_ref[pl.ds(MEMBERS, FACTS), lanes]],
            axis=0,
        ).astype(F32)
        beyond = beyond_ref[:, lanes].astype(F32)
        first = jnp.where(lane < SLOTS, here, pltpu.roll(beyond, SLOTS, 1))
        second = jnp.where(lane < SLOTS, pltpu.roll(here, SLOTS, 1), beyond)
        cat_ref[:, pl.ds(batch * BATCH_LANES, 2 * SLOTS)] = first.astype(BF16)
        cat_ref[:, pl.ds(batch * BATCH_LANES + 2 * SLOTS, 2 * SLOTS)] = second.astype(BF16)


def weights_of(columns, datum, noise, live):
    mean = jnp.sum(columns, axis=0, keepdims=True) * (1.0 / MEMBERS)
    pert = columns - mean
    variance = jnp.sum(pert * pert, axis=0, keepdims=True) / (MEMBERS - 1)
    denominator = jnp.where(live > 0.0, variance + noise, 1.0)
    factor = 1.0 / (1.0 + jnp.sqrt(noise / denominator))
    return pert, live * (datum - mean) / denominator, live * factor / denominator


def positions(masks):
    rows, lanes = masks.shape
    before = lax.broadcasted_iota(jnp.int32, (128, 128), 0)
    after = lax.broadcasted_iota(jnp.int32, (128, 128), 1)
    triangle = jnp.where(before < after, 1.0, 0.0).astype(BF16)
    total = jnp.zeros((rows, 1), F32)
    parts = []
    for start in range(0, lanes, 128):
        block = masks[:, start : start + 128]
        rank = jnp.dot(block.astype(BF16), triangle, preferred_element_type=F32) + total
        parts.append(jnp.where(block > 0.0, rank, -1.0))
        total = total + jnp.sum(block, axis=1, keepdims=True)
    return jnp.concatenate(parts, axis=1), total


def taper(square):
    inverse = lax.rsqrt(jnp.maximum(square, 1.0))
    distance = square * inverse
    inside = ((distance * (-0.25 / 1024.0) + 0.5 / 256.0) * distance + 0.625 / 64.0) * distance
    inside = (inside - 5.0 / 48.0) * square + 1.0
    left = jnp.maximum(8.0 - distance, 0.0)
    left = left * left
    outside = (distance * (0.125 / 1536.0) + 1.0 / 1536.0) * distance - 1.0 / 1536.0
    outside = outside * inverse * (left * left)
    return jnp.where(square <= 16.0, inside, outside)


def table_of(pert, mean_weight, pert_weight, row, col, level):
    high, low = split(pert)
    tail = [row.astype(F32), (col & ~127).astype(F32), (col & 127).astype(F32), level]
    for weight in (mean_weight, pert_weight):
        weight_high, weight_low = split(weight)
        tail += [weight_high.astype(F32), weight_low.astype(F32)]
    return jnp.concatenate([high, low, stack_rows(tail, 16).astype(BF16)], axis=0)


def chosen_records(ranks, bases, counts, table):
    parts = []
    for index, (base, count) in enumerate(zip(bases, counts)):
        place = lax.broadcasted_iota(jnp.int32, (count, 1), 0).astype(F32) + base
        parts.append(jnp.where(ranks[index : index + 1] == place, 1.0, 0.0).astype(BF16))
    chooser = jnp.concatenate(parts, axis=0)
    return lax.dot_general(chooser, table, (((1,), (1,)), ((), ())), preferred_element_type=F32)


def open_records(records):
    pert = records[:, : 2 * MEMBERS].astype(BF16)
    tail = records[:, 2 * MEMBERS :]
    row = tail[:, 0:1]
    col = tail[:, 1:2] + tail[:, 2:3]
    level = tail[:, 3:4]
    mean_weight = tail[:, 4:5] + tail[:, 5:6]
    pert_weight = tail[:, 6:7] + tail[:, 7:8]
    step = mean_weight - pert_weight * (records[:, :MEMBERS] + records[:, MEMBERS : 2 * MEMBERS])
    return pert, row, col, level, step * (1.0 / (MEMBERS - 1))


def halves(gain):
    high, low = split(gain)
    return jnp.concatenate([high, high, low], axis=0)


def advance(step, gain):
    high, low = split(step)
    return lax.dot_general(
        jnp.concatenate([high, low, high], axis=0),
        gain,
        (((0,), (0,)), ((), ())),
        preferred_element_type=F32,
    )


def region_step(records, strip, matched):
    pert, row, col, level, step = open_records(records)
    lane = lax.broadcasted_iota(jnp.int32, (1, STRIP), 1).astype(F32) + strip * STRIP
    across = col - lane
    across = across * across
    tile = jnp.floor(row * (1.0 / SPAN_NORTH))
    tapers = []
    for line in range(ROWS):
        down = row - float(line)
        tapers.append(taper(across + down * down))
    for target in range(LEVELS):
        factor = jnp.where(level == target, 1.0, 0.5)
        factors = [
            jnp.where(jnp.abs(tile - part) <= 1.0, factor, 0.0) for part in range(ROWS // SPAN_NORTH)
        ]
        weight = jnp.concatenate(
            [tapers[line] * factors[line // SPAN_NORTH] for line in range(ROWS)], axis=1
        )
        lanes = pl.ds(target * ROWS * STRIP, ROWS * STRIP)
        cells = matched(strip, lanes)
        if cells.shape[0] > 2 * MEMBERS:
            three = jnp.concatenate([pert, pert[:, :MEMBERS]], axis=1)
            covariance = jnp.dot(three, cells, preferred_element_type=F32)
        else:
            covariance = jnp.dot(pert, cells, preferred_element_type=F32)
        yield lanes, advance(step, halves(weight * covariance))


def chunks_of(total, size):
    return (jnp.max(total).astype(jnp.int32) + (size - 1)) // size


def rows_of(cats, rows, batch):
    parts = []
    for index, cat in enumerate(cats):
        start, count = batch * BATCH_LANES, BATCH_LANES
        if batch == 1 and index != 1:
            start, count = start + (2 * SLOTS if index == 0 else 0), 2 * SLOTS
        parts.append(cat[rows, pl.ds(start, count)])
    return jnp.concatenate(parts, axis=1)


def facts_of(cats, batch, place_ref):
    facts = rows_of(cats, pl.ds(MEMBERS, FACTS), batch).astype(F32)
    datum = facts[0:1] + facts[1:2] + facts[2:3]
    noise = facts[3:4] + facts[4:5] + facts[5:6]
    col = (facts[6:7] * 128.0 + facts[7:8]).astype(jnp.int32) - place_ref[4]
    row = facts[8:9].astype(jnp.int32) - place_ref[3]
    return datum, noise, col, row, facts[9:10], facts[10:11]


def masks_of(col, row, live):
    masks = []
    for strip in range(STRIPS):
        west = strip * STRIP - REACH
        inside = (col > west) & (col < west + STRIP + 2 * REACH - 1)
        inside = inside & (row >= -SPAN_NORTH) & (row < ROWS + SPAN_NORTH)
        masks.append(jnp.where(inside, live, 0.0))
    inside = (col > -2 * REACH) & (col < HALF + 2 * REACH - 1)
    masks.append(jnp.where(inside, live, 0.0))
    return stack_rows(masks, 8)


def arrange_kernel(strip, field_ref, cells_ref, wide):
    wide[...] = field_ref[:, strip * STRIP : (strip + 1) * STRIP].astype(F32)
    for line in range(LINES):
        piece = wide[pl.ds(line, MEMBERS, stride=LINES), :]
        cells_ref[:, pl.ds(line * STRIP, STRIP)] = piece.astype(BF16)


def analysis_kernel(place_ref, west_ref, east_ref, north_ref, here_ref, south_ref, message_ref, *scratch):
    refs = (place_ref, (west_ref, east_ref), (north_ref, here_ref, south_ref), message_ref, *scratch)
    more = analysis(False, *refs)

    @pl.when(more)
    def _():
        analysis(True, *refs)


def analysis(loops, place_ref, cells, cats, message_ref, wide, state, source, site_state):
    sizes = [CHUNK] * STRIPS
    pieces = [slice(strip * CHUNK, (strip + 1) * CHUNK) for strip in range(STRIPS)]
    members = pl.ds(0, MEMBERS)

    datum, noise, col, row, level, live = facts_of(cats, 0, place_ref)
    datum_1, noise_1, col_1, row_1, level_1, live_1 = facts_of(cats, 1, place_ref)
    ranks, total = positions(masks_of(col, row, live))
    ranks_1, total_1 = positions(masks_of(col_1, row_1, live_1))
    chunks = chunks_of(total[:STRIPS], CHUNK)
    chunks_1 = chunks_of(total_1[:STRIPS], CHUNK)
    site_chunks = chunks_of(total[STRIPS : STRIPS + 1], SITE_CHUNK)

    first = rows_of(cats, members, 0).astype(F32)
    pert, mean_weight, pert_weight = weights_of(first, datum, noise, live)
    table = table_of(pert, mean_weight, pert_weight, row, col, level)
    records = chosen_records(ranks, [0.0] * (STRIPS + 1), sizes + [SITE_CHUNK], table)

    sites = rows_of(cats, members, 1)
    site_row = row_1.astype(F32)
    site_col = col_1.astype(F32)
    site_tile = (row_1 >> 2).astype(F32)

    def site_step(records):
        obs, obs_row, obs_col, obs_level, step = open_records(records)
        down = obs_row - site_row
        across = obs_col - site_col
        weight = taper(down * down + across * across)
        weight = weight * jnp.where(obs_level == level_1, 1.0, 0.5)
        obs_tile = jnp.floor(obs_row * (1.0 / SPAN_NORTH))
        weight = jnp.where(jnp.abs(obs_tile - site_tile) <= 1.0, weight, 0.0)
        covariance = jnp.dot(obs, jnp.concatenate([sites, sites], axis=0), preferred_element_type=F32)
        return advance(step, halves(weight * covariance))

    after = sites.astype(F32) + site_step(records[STRIPS * CHUNK :])

    def more_sites(index, carry):
        base = (index * SITE_CHUNK).astype(F32)
        more = chosen_records(ranks[STRIPS : STRIPS + 1], [base], [SITE_CHUNK], table)
        site_state[...] = site_state[...] + site_step(more)
        return carry

    if loops:
        site_state[...] = after
        lax.fori_loop(1, site_chunks, more_sites, 0)
        after = site_state[...]

    def more_cells(ranks, table, matched):
        def one(index, carry):
            base = (index * CHUNK).astype(F32)
            more = chosen_records(ranks, [base] * STRIPS, sizes, table)
            for strip in range(STRIPS):
                for lanes, moved in region_step(more[pieces[strip]], strip, matched):
                    state[strip, :, lanes] = state[strip, :, lanes] + moved
            return carry

        return one

    def cells_of(strip, lanes):
        once = cells[strip][:, lanes]
        return jnp.concatenate([once, once], axis=0)

    for strip in range(STRIPS):
        for lanes, moved in region_step(records[pieces[strip]], strip, cells_of):
            state[strip, :, lanes] = cells[strip][:, lanes].astype(F32) + moved
    if loops:
        lax.fori_loop(1, chunks, more_cells(ranks, table, cells_of), 0)

    pert, mean_weight, pert_weight = weights_of(after, datum_1, noise_1, live_1)
    table_1 = table_of(pert, mean_weight, pert_weight, row_1, col_1, level_1)
    records_1 = chosen_records(ranks_1, [0.0] * STRIPS, sizes, table_1)

    def split_cells(strip, lanes):
        high, low = split(state[strip, :, lanes])
        if loops:
            source[strip, :MEMBERS, lanes] = high
            source[strip, MEMBERS:, lanes] = low
        return jnp.concatenate([high, high, low], axis=0)

    def source_of(strip, lanes):
        high = source[strip, :MEMBERS, lanes]
        return jnp.concatenate([high, high, source[strip, MEMBERS:, lanes]], axis=0)

    for strip in range(STRIPS):
        for lanes, moved in region_step(records_1[pieces[strip]], strip, split_cells):
            if loops:
                state[strip, :, lanes] = state[strip, :, lanes] + moved
                continue
            done = state[strip, :, lanes] + moved
            for line in range(ROWS):
                place = pl.ds(lanes.start // STRIP + line, MEMBERS, stride=LINES)
                wide[strip, place, :] = done[:, line * STRIP : (line + 1) * STRIP]
    if loops:
        lax.fori_loop(1, chunks_1, more_cells(ranks_1, table_1, source_of), 0)
        for strip in range(STRIPS):
            for line in range(LINES):
                wide[strip, pl.ds(line, MEMBERS, stride=LINES), :] = state[strip, :, pl.ds(line * STRIP, STRIP)]
    for part in range(STRIPS):
        message_ref[:, part * STRIP : (part + 1) * STRIP] = wide[part].astype(BF16)
    return (jnp.maximum(chunks, chunks_1) > 1) | (site_chunks > 1)


def call(kernel, shape, operands, scratch=(), scalars=0, flops=0, moved=1 << 18):
    smem = pl.BlockSpec(memory_space=pltpu.SMEM)
    vmem = pl.BlockSpec(memory_space=pltpu.VMEM)
    return pl.pallas_call(
        kernel,
        out_shape=jax.ShapeDtypeStruct(shape, BF16),
        in_specs=[smem if index < scalars else vmem for index in range(len(operands))],
        out_specs=vmem,
        scratch_shapes=list(scratch),
        compiler_params=pltpu.CompilerParams(vmem_limit_bytes=VMEM_LIMIT),
        cost_estimate=pl.CostEstimate(flops=flops, bytes_accessed=moved, transcendentals=0),
    )(*operands)


MESSAGE = (MEMBERS * LINES, HALF)


def pack(field):
    return call(pack_kernel, MESSAGE, (field,), moved=1 << 20)


def unpack(message):
    return call(unpack_kernel, (LEVELS, CHIPS * ROWS, SPAN_EAST), (message,), moved=1 << 20)


def state_facts(place, datum, noise, point, count):
    smem = pl.BlockSpec(memory_space=pltpu.SMEM)
    vmem = pl.BlockSpec(memory_space=pltpu.VMEM)
    return pl.pallas_call(
        facts_kernel,
        out_shape=jax.ShapeDtypeStruct((FACTS, 2 * SLOTS), BF16),
        in_specs=[smem, vmem, vmem, vmem, smem],
        out_specs=vmem,
        compiler_params=pltpu.CompilerParams(vmem_limit_bytes=VMEM_LIMIT),
    )(place, datum, noise, point, count)


def pick(place, field, own, other):
    scratch = [pltpu.VMEM((2, MEMBERS * LINES, 2 * SLOTS), F32)]
    return call(
        pick_kernel, (PACKET, 4 * SLOTS), (place, field, own, other), scratch, 1, 1 << 27, 1 << 19
    )


def merge(own, other, beyond):
    return call(merge_kernel, (PACKET, 2 * BATCH_LANES), (own, other, beyond))


def arrange(field, strip):
    kernel = functools.partial(arrange_kernel, strip)
    scratch = [pltpu.VMEM((MEMBERS * LINES, STRIP), F32)]
    return call(kernel, (MEMBERS, LINES * STRIP), (field,), scratch, moved=1 << 19)


def analyse(place, west, east, north, here, south):
    scratch = [
        pltpu.VMEM((STRIPS, MEMBERS * LINES, STRIP), F32),
        pltpu.VMEM((STRIPS, MEMBERS, LINES * STRIP), F32),
        pltpu.VMEM((STRIPS, 2 * MEMBERS, LINES * STRIP), BF16),
        pltpu.VMEM((MEMBERS, 2 * BATCH_LANES), F32),
    ]
    return call(
        analysis_kernel, MESSAGE, (place, west, east, north, here, south), scratch, 1, 1 << 30, 1 << 20
    )


def swap_cores(block):
    return lax.ppermute(block, "mem", [(i, i ^ 1) for i in range(lax.axis_size("mem"))])


def swap_beyond(block):
    rows, columns = lax.axis_size("mem"), lax.axis_size("tile")
    route = []
    for row in range(0, rows, 2):
        for column in range(columns - 1):
            west, east = (row + 1) * columns + column, row * columns + column + 1
            route += [(west, east), (east, west)]
    return lax.ppermute(block, ("mem", "tile"), route)


def from_behind(block, distance):
    size = lax.axis_size("mem")
    route = [(i - distance, i) for i in range(size) if 0 <= i - distance < size]
    return lax.ppermute(block, "mem", route)


def on_device(members, datum, noise, point, count):
    row = lax.axis_index("mem")
    column = lax.axis_index("tile")
    half = row % 2
    place = jnp.stack(
        [row * SPAN_NORTH, column * SPAN_EAST, half, (row // 2) * ROWS, column * SPAN_EAST + half * HALF]
    ).astype(jnp.int32)
    message = pack(members[0])
    field = lax.all_to_all(message, "mem", split_axis=0, concat_axis=0, tiled=True)
    facts = state_facts(place, datum, noise, point, count.reshape(2))
    packet = pick(place, field, facts, swap_cores(facts))
    field, packet = lax.optimization_barrier((field, packet))
    other = swap_cores(packet)
    west, packet = lax.optimization_barrier((arrange(field, 0), packet))
    here = merge(packet, other, swap_beyond(packet))
    field, here = lax.optimization_barrier((field, here))
    north = from_behind(here, 2)
    east, here = lax.optimization_barrier((arrange(field, 1), here))
    south = from_behind(here, -2)
    message = analyse(place, west, east, north, here, south)
    message = lax.all_to_all(message, "mem", split_axis=0, concat_axis=0, tiled=True)
    return unpack(message)[None]


def solution(mesh):
    return jax.shard_map(
        on_device,
        mesh=mesh,
        in_specs=(
            P("mem", None, None, "tile"),
            P(None, "mem", "tile", None),
            P(None, "mem", "tile", None),
            P(None, "mem", "tile", None),
            P(None, "mem", "tile"),
        ),
        out_specs=P("mem", None, None, "tile"),
        check_vma=False,
    )
```

```python
import functools

import jax
import jax.numpy as jnp
from jax import lax
from jax.experimental import pallas as pl
from jax.experimental.pallas import tpu as pltpu
from jax.sharding import PartitionSpec as P

MEMBERS = 64
LEVELS = 2
SPAN_NORTH = 4
SPAN_EAST = 512
SLOTS = 64
CHIPS = 32
CHIP_LINE = 8
ROWS = 2 * SPAN_NORTH
LINES = LEVELS * ROWS
HALF = SPAN_EAST // 2
STRIP = 128
STRIPS = HALF // STRIP
REACH = 8
CHUNK = 64
SITE_CHUNK = 160
FACTS = 16
PACKET = MEMBERS + FACTS
BATCH_LANES = 4 * SLOTS
F32 = jnp.float32
BF16 = jnp.bfloat16
VMEM_LIMIT = 48 * 1024 * 1024


def chip_of(region):
    line, place = divmod(region, CHIP_LINE)
    return line * CHIP_LINE + (CHIP_LINE - 1 - place if line % 2 else place)


def split(values):
    high = values.astype(BF16)
    return high, (values - high.astype(F32)).astype(BF16)


def pack_kernel(field_ref, message_ref):
    for group in range(CHIPS // 2):
        upper, lower = (
            field_ref[level, pl.ds(2 * ROWS * group, 2 * ROWS), :].astype(F32) for level in range(LEVELS)
        )
        for chip in range(2):
            rows = slice(chip * ROWS, (chip + 1) * ROWS)
            for half in range(2):
                lanes = slice(half * HALF, (half + 1) * HALF)
                place = (2 * chip_of(2 * group + chip) + half) * LINES
                message_ref[pl.ds(place, LINES), :] = jnp.concatenate(
                    [upper[rows, lanes], lower[rows, lanes]], axis=0
                ).astype(BF16)


def unpack_kernel(message_ref, field_ref):
    for group in range(CHIPS // 2):
        for half in range(2):
            lanes = pl.ds(half * HALF, HALF)
            first, second = (
                message_ref[pl.ds((2 * chip_of(2 * group + chip) + half) * LINES, LINES), :].astype(F32)
                for chip in range(2)
            )
            for level in range(LEVELS):
                rows = slice(level * ROWS, (level + 1) * ROWS)
                field_ref[level, pl.ds(2 * ROWS * group, 2 * ROWS), lanes] = jnp.concatenate(
                    [first[rows], second[rows]], axis=0
                ).astype(BF16)


def parts_of(values):
    high = values.astype(BF16).astype(F32)
    rest = values - high
    middle = rest.astype(BF16).astype(F32)
    return [high, middle, rest - middle]


def stack_rows(lines, count):
    shape = (count, lines[0].shape[1])
    rows = lax.broadcasted_iota(jnp.int32, shape, 0)
    block = jnp.zeros(shape, F32)
    for index, line in enumerate(lines):
        block = jnp.where(rows == index, line, block)
    return block


def facts_kernel(place_ref, datum_ref, noise_ref, point_ref, count_ref, facts_ref):
    lane = lax.broadcasted_iota(jnp.int32, (1, 2 * SLOTS), 1)

    def both(ref):
        first = jnp.concatenate([ref[0, 0], ref[0, 0]], axis=1)
        second = jnp.concatenate([ref[1, 0], ref[1, 0]], axis=1)
        return jnp.where(lane < SLOTS, first, second)

    point = both(point_ref)
    count = jnp.where(lane < SLOTS, count_ref[0], count_ref[1])
    col = place_ref[1] + (point & (SPAN_EAST - 1))
    row = place_ref[0] + ((point >> 9) & (SPAN_NORTH - 1))
    live = jnp.where((lane & (SLOTS - 1)) < count, 1.0, 0.0)
    lines = parts_of(both(datum_ref)) + parts_of(both(noise_ref))
    lines += [(col >> 7).astype(F32), (col & 127).astype(F32), row.astype(F32), (point >> 11).astype(F32), live]
    facts_ref[...] = stack_rows(lines, FACTS).astype(BF16)


def pick_kernel(place_ref, field_ref, own_ref, other_ref, packet_ref, scratch):
    own = own_ref[...].astype(F32)
    other = other_ref[...].astype(F32)
    half = place_ref[2]
    first = jnp.where(half == 0, own, other)
    second = jnp.where(half == 0, other, own)
    lane = lax.broadcasted_iota(jnp.int32, first.shape, 1)
    batches = (
        jnp.where(lane < SLOTS, first, pltpu.roll(second, SLOTS, 1)),
        jnp.where(lane < SLOTS, pltpu.roll(first, SLOTS, 1), second),
    )
    place = lax.broadcasted_iota(jnp.int32, (HALF, 2 * SLOTS), 0)
    choosers, lines = [], []
    for facts in batches:
        col = (facts[6:7] * 128.0 + facts[7:8]).astype(jnp.int32) - place_ref[4]
        lines.append((facts[9:10] * ROWS + facts[8:9]).astype(jnp.int32) - place_ref[3])
        choosers.append(jnp.where(place == col, 1.0, 0.0).astype(BF16))
    values = jnp.dot(field_ref[...], jnp.concatenate(choosers, axis=1), preferred_element_type=F32)
    for batch in range(2):
        lanes = pl.ds(batch * 2 * SLOTS, 2 * SLOTS)
        scratch[batch] = values[:, batch * 2 * SLOTS : (batch + 1) * 2 * SLOTS]
        total = jnp.zeros((MEMBERS, 2 * SLOTS), F32)
        for index in range(LINES):
            block = scratch[batch, pl.ds(index, MEMBERS, stride=LINES), :]
            total = total + jnp.where(lines[batch] == index, block, 0.0)
        packet_ref[pl.ds(0, MEMBERS), lanes] = total.astype(BF16)
        packet_ref[pl.ds(MEMBERS, FACTS), lanes] = batches[batch].astype(BF16)


def merge_kernel(own_ref, other_ref, beyond_ref, cat_ref):
    lane = lax.broadcasted_iota(jnp.int32, (PACKET, 2 * SLOTS), 1)
    for batch in range(2):
        lanes = pl.ds(batch * 2 * SLOTS, 2 * SLOTS)
        members = pl.ds(0, MEMBERS)
        here = jnp.concatenate(
            [own_ref[members, lanes] + other_ref[members, lanes], own_ref[pl.ds(MEMBERS, FACTS), lanes]],
            axis=0,
        ).astype(F32)
        beyond = beyond_ref[:, lanes].astype(F32)
        first = jnp.where(lane < SLOTS, here, pltpu.roll(beyond, SLOTS, 1))
        second = jnp.where(lane < SLOTS, pltpu.roll(here, SLOTS, 1), beyond)
        cat_ref[:, pl.ds(batch * BATCH_LANES, 2 * SLOTS)] = first.astype(BF16)
        cat_ref[:, pl.ds(batch * BATCH_LANES + 2 * SLOTS, 2 * SLOTS)] = second.astype(BF16)


def weights_of(columns, datum, noise, live):
    mean = jnp.sum(columns, axis=0, keepdims=True) * (1.0 / MEMBERS)
    pert = columns - mean
    variance = jnp.sum(pert * pert, axis=0, keepdims=True) / (MEMBERS - 1)
    denominator = jnp.where(live > 0.0, variance + noise, 1.0)
    factor = 1.0 / (1.0 + jnp.sqrt(noise / denominator))
    return pert, live * (datum - mean) / denominator, live * factor / denominator


def positions(masks):
    rows, lanes = masks.shape
    before = lax.broadcasted_iota(jnp.int32, (128, 128), 0)
    after = lax.broadcasted_iota(jnp.int32, (128, 128), 1)
    triangle = jnp.where(before < after, 1.0, 0.0).astype(BF16)
    total = jnp.zeros((rows, 1), F32)
    parts = []
    for start in range(0, lanes, 128):
        block = masks[:, start : start + 128]
        rank = jnp.dot(block.astype(BF16), triangle, preferred_element_type=F32) + total
        parts.append(jnp.where(block > 0.0, rank, -1.0))
        total = total + jnp.sum(block, axis=1, keepdims=True)
    return jnp.concatenate(parts, axis=1), total


def taper(square):
    inverse = lax.rsqrt(jnp.maximum(square, 1.0))
    distance = square * inverse
    inside = ((distance * (-0.25 / 1024.0) + 0.5 / 256.0) * distance + 0.625 / 64.0) * distance
    inside = (inside - 5.0 / 48.0) * square + 1.0
    left = jnp.maximum(8.0 - distance, 0.0)
    left = left * left
    outside = (distance * (0.125 / 1536.0) + 1.0 / 1536.0) * distance - 1.0 / 1536.0
    outside = outside * inverse * (left * left)
    return jnp.where(square <= 16.0, inside, outside)


def table_of(pert, mean_weight, pert_weight, row, col, level):
    high, low = split(pert)
    tail = [row.astype(F32), (col & ~127).astype(F32), (col & 127).astype(F32), level]
    for weight in (mean_weight, pert_weight):
        weight_high, weight_low = split(weight)
        tail += [weight_high.astype(F32), weight_low.astype(F32)]
    return jnp.concatenate([high, low, stack_rows(tail, 16).astype(BF16)], axis=0)


def chosen_records(ranks, bases, counts, table):
    parts = []
    for index, (base, count) in enumerate(zip(bases, counts)):
        place = lax.broadcasted_iota(jnp.int32, (count, 1), 0).astype(F32) + base
        parts.append(jnp.where(ranks[index : index + 1] == place, 1.0, 0.0).astype(BF16))
    chooser = jnp.concatenate(parts, axis=0)
    return lax.dot_general(chooser, table, (((1,), (1,)), ((), ())), preferred_element_type=F32)


def open_records(records):
    pert = records[:, : 2 * MEMBERS].astype(BF16)
    tail = records[:, 2 * MEMBERS :]
    row = tail[:, 0:1]
    col = tail[:, 1:2] + tail[:, 2:3]
    level = tail[:, 3:4]
    mean_weight = tail[:, 4:5] + tail[:, 5:6]
    pert_weight = tail[:, 6:7] + tail[:, 7:8]
    step = mean_weight - pert_weight * (records[:, :MEMBERS] + records[:, MEMBERS : 2 * MEMBERS])
    return pert, row, col, level, step * (1.0 / (MEMBERS - 1))


def halves(gain):
    high, low = split(gain)
    return jnp.concatenate([high, high, low], axis=0)


def advance(step, gain):
    high, low = split(step)
    return lax.dot_general(
        jnp.concatenate([high, low, high], axis=0),
        gain,
        (((0,), (0,)), ((), ())),
        preferred_element_type=F32,
    )


def region_step(records, strip, matched):
    pert, row, col, level, step = open_records(records)
    lane = lax.broadcasted_iota(jnp.int32, (1, STRIP), 1).astype(F32) + strip * STRIP
    across = col - lane
    across = across * across
    tile = jnp.floor(row * (1.0 / SPAN_NORTH))
    tapers = []
    for line in range(ROWS):
        down = row - float(line)
        tapers.append(taper(across + down * down))
    for target in range(LEVELS):
        factor = jnp.where(level == target, 1.0, 0.5)
        factors = [
            jnp.where(jnp.abs(tile - part) <= 1.0, factor, 0.0) for part in range(ROWS // SPAN_NORTH)
        ]
        weight = jnp.concatenate(
            [tapers[line] * factors[line // SPAN_NORTH] for line in range(ROWS)], axis=1
        )
        lanes = pl.ds(target * ROWS * STRIP, ROWS * STRIP)
        cells = matched(strip, lanes)
        if cells.shape[0] > 2 * MEMBERS:
            three = jnp.concatenate([pert, pert[:, :MEMBERS]], axis=1)
            covariance = jnp.dot(three, cells, preferred_element_type=F32)
        else:
            covariance = jnp.dot(pert, cells, preferred_element_type=F32)
        yield lanes, advance(step, halves(weight * covariance))


def chunks_of(total, size):
    return (jnp.max(total).astype(jnp.int32) + (size - 1)) // size


def rows_of(cats, rows, batch, place_ref):
    parts = []
    for index, cat in enumerate(cats):
        start, count = batch * BATCH_LANES, BATCH_LANES
        if batch == 1 and index != 1:
            north = place_ref[5] if index == 0 else 1 - place_ref[5]
            start, count = pl.multiple_of(start + north * (2 * SLOTS), 2 * SLOTS), 2 * SLOTS
        parts.append(cat[rows, pl.ds(start, count)])
    return jnp.concatenate(parts, axis=1)


def facts_of(cats, batch, place_ref):
    facts = rows_of(cats, pl.ds(MEMBERS, FACTS), batch, place_ref).astype(F32)
    datum = facts[0:1] + facts[1:2] + facts[2:3]
    noise = facts[3:4] + facts[4:5] + facts[5:6]
    col = (facts[6:7] * 128.0 + facts[7:8]).astype(jnp.int32) - place_ref[4]
    row = facts[8:9].astype(jnp.int32) - place_ref[3]
    return datum, noise, col, row, facts[9:10], facts[10:11]


def masks_of(col, row, live):
    masks = []
    for strip in range(STRIPS):
        west = strip * STRIP - REACH
        inside = (col > west) & (col < west + STRIP + 2 * REACH - 1)
        inside = inside & (row >= -SPAN_NORTH) & (row < ROWS + SPAN_NORTH)
        masks.append(jnp.where(inside, live, 0.0))
    inside = (col > -2 * REACH) & (col < HALF + 2 * REACH - 1)
    masks.append(jnp.where(inside, live, 0.0))
    return stack_rows(masks, 8)


def arrange_kernel(strip, field_ref, cells_ref, wide):
    wide[...] = field_ref[:, strip * STRIP : (strip + 1) * STRIP].astype(F32)
    for line in range(LINES):
        piece = wide[pl.ds(line, MEMBERS, stride=LINES), :]
        cells_ref[:, pl.ds(line * STRIP, STRIP)] = piece.astype(BF16)


def analysis_kernel(place_ref, west_ref, east_ref, next_ref, here_ref, last_ref, message_ref, *scratch):
    refs = (place_ref, (west_ref, east_ref), (next_ref, here_ref, last_ref), message_ref, *scratch)
    more = analysis(False, *refs)

    @pl.when(more)
    def _():
        analysis(True, *refs)


def analysis(loops, place_ref, cells, cats, message_ref, wide, state, source, site_state):
    sizes = [CHUNK] * STRIPS
    pieces = [slice(strip * CHUNK, (strip + 1) * CHUNK) for strip in range(STRIPS)]
    members = pl.ds(0, MEMBERS)

    datum, noise, col, row, level, live = facts_of(cats, 0, place_ref)
    datum_1, noise_1, col_1, row_1, level_1, live_1 = facts_of(cats, 1, place_ref)
    ranks, total = positions(masks_of(col, row, live))
    ranks_1, total_1 = positions(masks_of(col_1, row_1, live_1))
    chunks = chunks_of(total[:STRIPS], CHUNK)
    chunks_1 = chunks_of(total_1[:STRIPS], CHUNK)
    site_chunks = chunks_of(total[STRIPS : STRIPS + 1], SITE_CHUNK)

    first = rows_of(cats, members, 0, place_ref).astype(F32)
    pert, mean_weight, pert_weight = weights_of(first, datum, noise, live)
    table = table_of(pert, mean_weight, pert_weight, row, col, level)
    records = chosen_records(ranks, [0.0] * (STRIPS + 1), sizes + [SITE_CHUNK], table)

    sites = rows_of(cats, members, 1, place_ref)
    site_row = row_1.astype(F32)
    site_col = col_1.astype(F32)
    site_tile = (row_1 >> 2).astype(F32)

    def site_step(records):
        obs, obs_row, obs_col, obs_level, step = open_records(records)
        down = obs_row - site_row
        across = obs_col - site_col
        weight = taper(down * down + across * across)
        weight = weight * jnp.where(obs_level == level_1, 1.0, 0.5)
        obs_tile = jnp.floor(obs_row * (1.0 / SPAN_NORTH))
        weight = jnp.where(jnp.abs(obs_tile - site_tile) <= 1.0, weight, 0.0)
        covariance = jnp.dot(obs, jnp.concatenate([sites, sites], axis=0), preferred_element_type=F32)
        return advance(step, halves(weight * covariance))

    after = sites.astype(F32) + site_step(records[STRIPS * CHUNK :])

    def more_sites(index, carry):
        base = (index * SITE_CHUNK).astype(F32)
        more = chosen_records(ranks[STRIPS : STRIPS + 1], [base], [SITE_CHUNK], table)
        site_state[...] = site_state[...] + site_step(more)
        return carry

    if loops:
        site_state[...] = after
        lax.fori_loop(1, site_chunks, more_sites, 0)
        after = site_state[...]

    def more_cells(ranks, table, matched):
        def one(index, carry):
            base = (index * CHUNK).astype(F32)
            more = chosen_records(ranks, [base] * STRIPS, sizes, table)
            for strip in range(STRIPS):
                for lanes, moved in region_step(more[pieces[strip]], strip, matched):
                    state[strip, :, lanes] = state[strip, :, lanes] + moved
            return carry

        return one

    def cells_of(strip, lanes):
        once = cells[strip][:, lanes]
        return jnp.concatenate([once, once], axis=0)

    for strip in range(STRIPS):
        for lanes, moved in region_step(records[pieces[strip]], strip, cells_of):
            state[strip, :, lanes] = cells[strip][:, lanes].astype(F32) + moved
    if loops:
        lax.fori_loop(1, chunks, more_cells(ranks, table, cells_of), 0)

    pert, mean_weight, pert_weight = weights_of(after, datum_1, noise_1, live_1)
    table_1 = table_of(pert, mean_weight, pert_weight, row_1, col_1, level_1)
    records_1 = chosen_records(ranks_1, [0.0] * STRIPS, sizes, table_1)

    def split_cells(strip, lanes):
        high, low = split(state[strip, :, lanes])
        if loops:
            source[strip, :MEMBERS, lanes] = high
            source[strip, MEMBERS:, lanes] = low
        return jnp.concatenate([high, high, low], axis=0)

    def source_of(strip, lanes):
        high = source[strip, :MEMBERS, lanes]
        return jnp.concatenate([high, high, source[strip, MEMBERS:, lanes]], axis=0)

    for strip in range(STRIPS):
        for lanes, moved in region_step(records_1[pieces[strip]], strip, split_cells):
            if loops:
                state[strip, :, lanes] = state[strip, :, lanes] + moved
                continue
            done = state[strip, :, lanes] + moved
            for line in range(ROWS):
                place = pl.ds(lanes.start // STRIP + line, MEMBERS, stride=LINES)
                wide[strip, place, :] = done[:, line * STRIP : (line + 1) * STRIP]
    if loops:
        lax.fori_loop(1, chunks_1, more_cells(ranks_1, table_1, source_of), 0)
        for strip in range(STRIPS):
            for line in range(LINES):
                wide[strip, pl.ds(line, MEMBERS, stride=LINES), :] = state[strip, :, pl.ds(line * STRIP, STRIP)]
    for part in range(STRIPS):
        message_ref[:, part * STRIP : (part + 1) * STRIP] = wide[part].astype(BF16)
    return (jnp.maximum(chunks, chunks_1) > 1) | (site_chunks > 1)


def call(kernel, shape, operands, scratch=(), scalars=0, flops=0, moved=1 << 18):
    smem = pl.BlockSpec(memory_space=pltpu.SMEM)
    vmem = pl.BlockSpec(memory_space=pltpu.VMEM)
    return pl.pallas_call(
        kernel,
        out_shape=jax.ShapeDtypeStruct(shape, BF16),
        in_specs=[smem if index < scalars else vmem for index in range(len(operands))],
        out_specs=vmem,
        scratch_shapes=list(scratch),
        compiler_params=pltpu.CompilerParams(vmem_limit_bytes=VMEM_LIMIT),
        cost_estimate=pl.CostEstimate(flops=flops, bytes_accessed=moved, transcendentals=0),
    )(*operands)


MESSAGE = (MEMBERS * LINES, HALF)


def pack(field):
    return call(pack_kernel, MESSAGE, (field,), moved=1 << 20)


def unpack(message):
    return call(unpack_kernel, (LEVELS, CHIPS * ROWS, SPAN_EAST), (message,), moved=1 << 20)


def state_facts(place, datum, noise, point, count):
    smem = pl.BlockSpec(memory_space=pltpu.SMEM)
    vmem = pl.BlockSpec(memory_space=pltpu.VMEM)
    return pl.pallas_call(
        facts_kernel,
        out_shape=jax.ShapeDtypeStruct((FACTS, 2 * SLOTS), BF16),
        in_specs=[smem, vmem, vmem, vmem, smem],
        out_specs=vmem,
        compiler_params=pltpu.CompilerParams(vmem_limit_bytes=VMEM_LIMIT),
    )(place, datum, noise, point, count)


def pick(place, field, own, other):
    scratch = [pltpu.VMEM((2, MEMBERS * LINES, 2 * SLOTS), F32)]
    return call(
        pick_kernel, (PACKET, 4 * SLOTS), (place, field, own, other), scratch, 1, 1 << 27, 1 << 19
    )


def merge(own, other, beyond):
    return call(merge_kernel, (PACKET, 2 * BATCH_LANES), (own, other, beyond))


def arrange(field, strip):
    kernel = functools.partial(arrange_kernel, strip)
    scratch = [pltpu.VMEM((MEMBERS * LINES, STRIP), F32)]
    return call(kernel, (MEMBERS, LINES * STRIP), (field,), scratch, moved=1 << 19)


def analyse(place, west, east, first, here, second):
    scratch = [
        pltpu.VMEM((STRIPS, MEMBERS * LINES, STRIP), F32),
        pltpu.VMEM((STRIPS, MEMBERS, LINES * STRIP), F32),
        pltpu.VMEM((STRIPS, 2 * MEMBERS, LINES * STRIP), BF16),
        pltpu.VMEM((MEMBERS, 2 * BATCH_LANES), F32),
    ]
    return call(
        analysis_kernel, MESSAGE, (place, west, east, first, here, second), scratch, 1, 1 << 30, 1 << 20
    )


def swap_cores(block):
    return lax.ppermute(block, "mem", [(i, i ^ 1) for i in range(lax.axis_size("mem"))])


def to_region(block, change):
    route = [(2 * k + h, 2 * chip_of(k) + (h ^ change)) for k in range(CHIPS) for h in range(2)]
    return lax.ppermute(block, "mem", route)


def swap_beyond(block):
    rows, columns = lax.axis_size("mem"), lax.axis_size("tile")
    route = []
    for row in range(0, rows, 2):
        for column in range(columns - 1):
            west, east = (row + 1) * columns + column, row * columns + column + 1
            route += [(west, east), (east, west)]
    return lax.ppermute(block, ("mem", "tile"), route)


def swap_regions(block, start):
    route = []
    for region in range(start, CHIPS - 1, 2):
        for half in range(2):
            one, two = 2 * chip_of(region) + half, 2 * chip_of(region + 1) + half
            route += [(one, two), (two, one)]
    return lax.ppermute(block, "mem", route)


def on_device(members, datum, noise, point, count):
    row = lax.axis_index("mem")
    column = lax.axis_index("tile")
    half = row % 2
    line, place = row // 2 // CHIP_LINE, row // 2 % CHIP_LINE
    region = line * CHIP_LINE + jnp.where(line % 2 == 1, CHIP_LINE - 1 - place, place)
    place = jnp.stack(
        [
            row * SPAN_NORTH,
            column * SPAN_EAST,
            half,
            region * ROWS,
            column * SPAN_EAST + half * HALF,
            region % 2,
        ]
    ).astype(jnp.int32)
    message = pack(members[0])
    field = lax.all_to_all(message, "mem", split_axis=0, concat_axis=0, tiled=True)
    facts = state_facts(place, datum, noise, point, count.reshape(2))
    packet = pick(place, field, to_region(facts, 0), to_region(facts, 1))
    field, packet = lax.optimization_barrier((field, packet))
    other = swap_cores(packet)
    west, packet = lax.optimization_barrier((arrange(field, 0), packet))
    here = merge(packet, other, swap_beyond(packet))
    field, here = lax.optimization_barrier((field, here))
    first = swap_regions(here, 0)
    east, here = lax.optimization_barrier((arrange(field, 1), here))
    second = swap_regions(here, 1)
    message = analyse(place, west, east, first, here, second)
    message = lax.all_to_all(message, "mem", split_axis=0, concat_axis=0, tiled=True)
    return unpack(message)[None]


def solution(mesh):
    return jax.shard_map(
        on_device,
        mesh=mesh,
        in_specs=(
            P("mem", None, None, "tile"),
            P(None, "mem", "tile", None),
            P(None, "mem", "tile", None),
            P(None, "mem", "tile", None),
            P(None, "mem", "tile"),
        ),
        out_specs=P("mem", None, None, "tile"),
        check_vma=False,
    )
```

```python
import jax
import jax.numpy as jnp
from jax import lax
from jax.experimental import pallas as pl
from jax.experimental.pallas import tpu as pltpu
from jax.sharding import PartitionSpec as P

MEMBERS = 64
LEVELS = 2
SPAN_NORTH = 4
SPAN_EAST = 512
SLOTS = 64
CHIPS = 32
ROWS = 2 * SPAN_NORTH
LINES = LEVELS * ROWS
HALF = SPAN_EAST // 2
STRIP = 128
STRIPS = HALF // STRIP
REACH = 8
CHUNK = 64
SITE_CHUNK = 160
FACTS = 16
PACKET = MEMBERS + FACTS
BATCH_LANES = 4 * SLOTS
F32 = jnp.float32
BF16 = jnp.bfloat16
VMEM_LIMIT = 48 * 1024 * 1024


def split(values):
    high = values.astype(BF16)
    return high, (values - high.astype(F32)).astype(BF16)


def pack_kernel(field_ref, message_ref):
    for group in range(CHIPS // 2):
        upper, lower = (
            field_ref[level, pl.ds(2 * ROWS * group, 2 * ROWS), :].astype(F32) for level in range(LEVELS)
        )
        for chip in range(2):
            rows = slice(chip * ROWS, (chip + 1) * ROWS)
            for half in range(2):
                lanes = slice(half * HALF, (half + 1) * HALF)
                place = (4 * group + 2 * chip + half) * LINES
                message_ref[pl.ds(place, LINES), :] = jnp.concatenate(
                    [upper[rows, lanes], lower[rows, lanes]], axis=0
                ).astype(BF16)


def unpack_kernel(message_ref, field_ref):
    for group in range(CHIPS // 2):
        for half in range(2):
            lanes = pl.ds(half * HALF, HALF)
            first, second = (
                message_ref[pl.ds((4 * group + 2 * chip + half) * LINES, LINES), :].astype(F32)
                for chip in range(2)
            )
            for level in range(LEVELS):
                rows = slice(level * ROWS, (level + 1) * ROWS)
                field_ref[level, pl.ds(2 * ROWS * group, 2 * ROWS), lanes] = jnp.concatenate(
                    [first[rows], second[rows]], axis=0
                ).astype(BF16)


def parts_of(values):
    high = values.astype(BF16).astype(F32)
    rest = values - high
    middle = rest.astype(BF16).astype(F32)
    return [high, middle, rest - middle]


def stack_rows(lines, count):
    shape = (count, lines[0].shape[1])
    rows = lax.broadcasted_iota(jnp.int32, shape, 0)
    block = jnp.zeros(shape, F32)
    for index, line in enumerate(lines):
        block = jnp.where(rows == index, line, block)
    return block


def facts_kernel(place_ref, datum_ref, noise_ref, point_ref, count_ref, facts_ref):
    lane = lax.broadcasted_iota(jnp.int32, (1, 2 * SLOTS), 1)

    def both(ref):
        first = jnp.concatenate([ref[0, 0], ref[0, 0]], axis=1)
        second = jnp.concatenate([ref[1, 0], ref[1, 0]], axis=1)
        return jnp.where(lane < SLOTS, first, second)

    point = both(point_ref)
    count = jnp.where(lane < SLOTS, count_ref[0], count_ref[1])
    col = place_ref[1] + (point & (SPAN_EAST - 1))
    row = place_ref[0] + ((point >> 9) & (SPAN_NORTH - 1))
    live = jnp.where((lane & (SLOTS - 1)) < count, 1.0, 0.0)
    lines = parts_of(both(datum_ref)) + parts_of(both(noise_ref))
    lines += [(col >> 7).astype(F32), (col & 127).astype(F32), row.astype(F32), (point >> 11).astype(F32), live]
    facts_ref[...] = stack_rows(lines, FACTS).astype(BF16)


def pick_kernel(place_ref, field_ref, own_ref, other_ref, packet_ref, scratch):
    own = own_ref[...].astype(F32)
    other = other_ref[...].astype(F32)
    half = place_ref[2]
    first = jnp.where(half == 0, own, other)
    second = jnp.where(half == 0, other, own)
    lane = lax.broadcasted_iota(jnp.int32, first.shape, 1)
    batches = (
        jnp.where(lane < SLOTS, first, pltpu.roll(second, SLOTS, 1)),
        jnp.where(lane < SLOTS, pltpu.roll(first, SLOTS, 1), second),
    )
    place = lax.broadcasted_iota(jnp.int32, (HALF, 2 * SLOTS), 0)
    choosers, lines = [], []
    for facts in batches:
        col = (facts[6:7] * 128.0 + facts[7:8]).astype(jnp.int32) - place_ref[4]
        lines.append((facts[9:10] * ROWS + facts[8:9]).astype(jnp.int32) - place_ref[3])
        choosers.append(jnp.where(place == col, 1.0, 0.0).astype(BF16))
    values = jnp.dot(field_ref[...], jnp.concatenate(choosers, axis=1), preferred_element_type=F32)
    for batch in range(2):
        lanes = pl.ds(batch * 2 * SLOTS, 2 * SLOTS)
        scratch[batch] = values[:, batch * 2 * SLOTS : (batch + 1) * 2 * SLOTS]
        total = jnp.zeros((MEMBERS, 2 * SLOTS), F32)
        for index in range(LINES):
            block = scratch[batch, pl.ds(index, MEMBERS, stride=LINES), :]
            total = total + jnp.where(lines[batch] == index, block, 0.0)
        packet_ref[pl.ds(0, MEMBERS), lanes] = total.astype(BF16)
        packet_ref[pl.ds(MEMBERS, FACTS), lanes] = batches[batch].astype(BF16)


def merge_kernel(place_ref, own_ref, other_ref, beyond_ref, here_ref, first_ref, second_ref):
    lane = lax.broadcasted_iota(jnp.int32, (PACKET, 2 * SLOTS), 1)
    odd = place_ref[5]
    for batch in range(2):
        lanes = pl.ds(batch * 2 * SLOTS, 2 * SLOTS)
        members = pl.ds(0, MEMBERS)
        here = jnp.concatenate(
            [own_ref[members, lanes] + other_ref[members, lanes], own_ref[pl.ds(MEMBERS, FACTS), lanes]],
            axis=0,
        ).astype(F32)
        beyond = beyond_ref[:, lanes].astype(F32)
        upper = jnp.where(lane < SLOTS, here, pltpu.roll(beyond, SLOTS, 1))
        lower = jnp.where(lane < SLOTS, pltpu.roll(here, SLOTS, 1), beyond)
        start = batch * BATCH_LANES
        here_ref[:, pl.ds(start, 2 * SLOTS)] = upper.astype(BF16)
        here_ref[:, pl.ds(start + 2 * SLOTS, 2 * SLOTS)] = lower.astype(BF16)
        if batch == 0:
            for ref in (first_ref, second_ref):
                ref[:, pl.ds(0, 2 * SLOTS)] = upper.astype(BF16)
                ref[:, pl.ds(2 * SLOTS, 2 * SLOTS)] = lower.astype(BF16)
        else:
            first_ref[:, pl.ds(start, 2 * SLOTS)] = jnp.where(odd == 0, lower, upper).astype(BF16)
            second_ref[:, pl.ds(start, 2 * SLOTS)] = jnp.where(odd == 0, upper, lower).astype(BF16)


def weights_of(columns, datum, noise, live):
    mean = jnp.sum(columns, axis=0, keepdims=True) * (1.0 / MEMBERS)
    pert = columns - mean
    variance = jnp.sum(pert * pert, axis=0, keepdims=True) / (MEMBERS - 1)
    denominator = jnp.where(live > 0.0, variance + noise, 1.0)
    factor = 1.0 / (1.0 + jnp.sqrt(noise / denominator))
    return pert, live * (datum - mean) / denominator, live * factor / denominator


def positions(masks):
    rows, lanes = masks.shape
    before = lax.broadcasted_iota(jnp.int32, (128, 128), 0)
    after = lax.broadcasted_iota(jnp.int32, (128, 128), 1)
    triangle = jnp.where(before < after, 1.0, 0.0).astype(BF16)
    total = jnp.zeros((rows, 1), F32)
    parts = []
    for start in range(0, lanes, 128):
        block = masks[:, start : start + 128]
        rank = jnp.dot(block.astype(BF16), triangle, preferred_element_type=F32) + total
        parts.append(jnp.where(block > 0.0, rank, -1.0))
        total = total + jnp.sum(block, axis=1, keepdims=True)
    return jnp.concatenate(parts, axis=1), total


def taper(square):
    inverse = lax.rsqrt(jnp.maximum(square, 1.0))
    distance = square * inverse
    inside = ((distance * (-0.25 / 1024.0) + 0.5 / 256.0) * distance + 0.625 / 64.0) * distance
    inside = (inside - 5.0 / 48.0) * square + 1.0
    left = jnp.maximum(8.0 - distance, 0.0)
    left = left * left
    outside = (distance * (0.125 / 1536.0) + 1.0 / 1536.0) * distance - 1.0 / 1536.0
    outside = outside * inverse * (left * left)
    return jnp.where(square <= 16.0, inside, outside)


def table_of(pert, mean_weight, pert_weight, row, col, level):
    high, low = split(pert)
    tail = [row.astype(F32), (col & ~127).astype(F32), (col & 127).astype(F32), level]
    for weight in (mean_weight, pert_weight):
        weight_high, weight_low = split(weight)
        tail += [weight_high.astype(F32), weight_low.astype(F32)]
    return jnp.concatenate([high, low, stack_rows(tail, 16).astype(BF16)], axis=0)


def chosen_records(ranks, bases, counts, table):
    parts = []
    for index, (base, count) in enumerate(zip(bases, counts)):
        place = lax.broadcasted_iota(jnp.int32, (count, 1), 0).astype(F32) + base
        parts.append(jnp.where(ranks[index : index + 1] == place, 1.0, 0.0).astype(BF16))
    chooser = jnp.concatenate(parts, axis=0)
    return lax.dot_general(chooser, table, (((1,), (1,)), ((), ())), preferred_element_type=F32)


def open_records(records):
    pert = records[:, : 2 * MEMBERS].astype(BF16)
    tail = records[:, 2 * MEMBERS :]
    row = tail[:, 0:1]
    col = tail[:, 1:2] + tail[:, 2:3]
    level = tail[:, 3:4]
    mean_weight = tail[:, 4:5] + tail[:, 5:6]
    pert_weight = tail[:, 6:7] + tail[:, 7:8]
    step = mean_weight - pert_weight * (records[:, :MEMBERS] + records[:, MEMBERS : 2 * MEMBERS])
    return pert, row, col, level, step * (1.0 / (MEMBERS - 1))


def halves(gain):
    high, low = split(gain)
    return jnp.concatenate([high, high, low], axis=0)


def advance(step, gain):
    high, low = split(step)
    return lax.dot_general(
        jnp.concatenate([high, low, high], axis=0),
        gain,
        (((0,), (0,)), ((), ())),
        preferred_element_type=F32,
    )


def region_step(records, strip, matched):
    pert, row, col, level, step = open_records(records)
    lane = lax.broadcasted_iota(jnp.int32, (1, STRIP), 1).astype(F32) + strip * STRIP
    across = col - lane
    across = across * across
    tile = jnp.floor(row * (1.0 / SPAN_NORTH))
    tapers = []
    for line in range(ROWS):
        down = row - float(line)
        tapers.append(taper(across + down * down))
    for target in range(LEVELS):
        factor = jnp.where(level == target, 1.0, 0.5)
        factors = [
            jnp.where(jnp.abs(tile - part) <= 1.0, factor, 0.0) for part in range(ROWS // SPAN_NORTH)
        ]
        weight = jnp.concatenate(
            [tapers[line] * factors[line // SPAN_NORTH] for line in range(ROWS)], axis=1
        )
        lanes = pl.ds(target * ROWS * STRIP, ROWS * STRIP)
        cells = matched(strip, lanes)
        if cells.shape[0] > 2 * MEMBERS:
            three = jnp.concatenate([pert, pert[:, :MEMBERS]], axis=1)
            covariance = jnp.dot(three, cells, preferred_element_type=F32)
        else:
            covariance = jnp.dot(pert, cells, preferred_element_type=F32)
        yield lanes, advance(step, halves(weight * covariance))


def chunks_of(total, size):
    return (jnp.max(total).astype(jnp.int32) + (size - 1)) // size


def rows_of(cats, rows, batch):
    parts = []
    for index, cat in enumerate(cats):
        count = 2 * SLOTS if batch == 1 and index != 1 else BATCH_LANES
        parts.append(cat[rows, pl.ds(batch * BATCH_LANES, count)])
    return jnp.concatenate(parts, axis=1)


def facts_of(cats, batch, place_ref):
    facts = rows_of(cats, pl.ds(MEMBERS, FACTS), batch).astype(F32)
    datum = facts[0:1] + facts[1:2] + facts[2:3]
    noise = facts[3:4] + facts[4:5] + facts[5:6]
    col = (facts[6:7] * 128.0 + facts[7:8]).astype(jnp.int32) - place_ref[4]
    row = facts[8:9].astype(jnp.int32) - place_ref[3]
    return datum, noise, col, row, facts[9:10], facts[10:11]


def masks_of(col, row, live):
    masks = []
    for strip in range(STRIPS):
        west = strip * STRIP - REACH
        inside = (col > west) & (col < west + STRIP + 2 * REACH - 1)
        inside = inside & (row >= -SPAN_NORTH) & (row < ROWS + SPAN_NORTH)
        masks.append(jnp.where(inside, live, 0.0))
    inside = (col > -2 * REACH) & (col < HALF + 2 * REACH - 1)
    masks.append(jnp.where(inside, live, 0.0))
    return stack_rows(masks, 8)


def arrange_kernel(field_ref, cells_ref, wide):
    for strip in range(STRIPS):
        wide[strip] = field_ref[:, strip * STRIP : (strip + 1) * STRIP].astype(F32)
    for strip in range(STRIPS):
        for line in range(LINES):
            piece = wide[strip, pl.ds(line, MEMBERS, stride=LINES), :]
            cells_ref[strip, :, pl.ds(line * STRIP, STRIP)] = piece.astype(BF16)


def analysis_kernel(place_ref, cells_ref, next_ref, here_ref, last_ref, message_ref, *scratch):
    refs = (place_ref, cells_ref, (next_ref, here_ref, last_ref), message_ref, *scratch)
    more = analysis(False, *refs)

    @pl.when(more)
    def _():
        analysis(True, *refs)


def analysis(loops, place_ref, cells, cats, message_ref, wide, state, source, site_state):
    sizes = [CHUNK] * STRIPS
    pieces = [slice(strip * CHUNK, (strip + 1) * CHUNK) for strip in range(STRIPS)]
    members = pl.ds(0, MEMBERS)

    datum, noise, col, row, level, live = facts_of(cats, 0, place_ref)
    datum_1, noise_1, col_1, row_1, level_1, live_1 = facts_of(cats, 1, place_ref)
    ranks, total = positions(masks_of(col, row, live))
    ranks_1, total_1 = positions(masks_of(col_1, row_1, live_1))
    chunks = chunks_of(total[:STRIPS], CHUNK)
    chunks_1 = chunks_of(total_1[:STRIPS], CHUNK)
    site_chunks = chunks_of(total[STRIPS : STRIPS + 1], SITE_CHUNK)

    first = rows_of(cats, members, 0).astype(F32)
    pert, mean_weight, pert_weight = weights_of(first, datum, noise, live)
    table = table_of(pert, mean_weight, pert_weight, row, col, level)
    records = chosen_records(ranks, [0.0] * (STRIPS + 1), sizes + [SITE_CHUNK], table)

    sites = rows_of(cats, members, 1)
    site_row = row_1.astype(F32)
    site_col = col_1.astype(F32)
    site_tile = (row_1 >> 2).astype(F32)

    def site_step(records):
        obs, obs_row, obs_col, obs_level, step = open_records(records)
        down = obs_row - site_row
        across = obs_col - site_col
        weight = taper(down * down + across * across)
        weight = weight * jnp.where(obs_level == level_1, 1.0, 0.5)
        obs_tile = jnp.floor(obs_row * (1.0 / SPAN_NORTH))
        weight = jnp.where(jnp.abs(obs_tile - site_tile) <= 1.0, weight, 0.0)
        covariance = jnp.dot(obs, jnp.concatenate([sites, sites], axis=0), preferred_element_type=F32)
        return advance(step, halves(weight * covariance))

    after = sites.astype(F32) + site_step(records[STRIPS * CHUNK :])

    def more_sites(index, carry):
        base = (index * SITE_CHUNK).astype(F32)
        more = chosen_records(ranks[STRIPS : STRIPS + 1], [base], [SITE_CHUNK], table)
        site_state[...] = site_state[...] + site_step(more)
        return carry

    if loops:
        site_state[...] = after
        lax.fori_loop(1, site_chunks, more_sites, 0)
        after = site_state[...]

    def more_cells(ranks, table, matched):
        def one(index, carry):
            base = (index * CHUNK).astype(F32)
            more = chosen_records(ranks, [base] * STRIPS, sizes, table)
            for strip in range(STRIPS):
                for lanes, moved in region_step(more[pieces[strip]], strip, matched):
                    state[strip, :, lanes] = state[strip, :, lanes] + moved
            return carry

        return one

    pert, mean_weight, pert_weight = weights_of(after, datum_1, noise_1, live_1)
    table_1 = table_of(pert, mean_weight, pert_weight, row_1, col_1, level_1)
    records_1 = chosen_records(ranks_1, [0.0] * STRIPS, sizes, table_1)

    def cells_of(strip, lanes):
        once = cells[strip, :, lanes]
        return jnp.concatenate([once, once], axis=0)

    for strip in range(STRIPS):
        for lanes, moved in region_step(records[pieces[strip]], strip, cells_of):
            state[strip, :, lanes] = cells[strip, :, lanes].astype(F32) + moved
    if loops:
        lax.fori_loop(1, chunks, more_cells(ranks, table, cells_of), 0)


    def split_cells(strip, lanes):
        high, low = split(state[strip, :, lanes])
        if loops:
            source[strip, :MEMBERS, lanes] = high
            source[strip, MEMBERS:, lanes] = low
        return jnp.concatenate([high, high, low], axis=0)

    def source_of(strip, lanes):
        high = source[strip, :MEMBERS, lanes]
        return jnp.concatenate([high, high, source[strip, MEMBERS:, lanes]], axis=0)

    for strip in range(STRIPS):
        for lanes, moved in region_step(records_1[pieces[strip]], strip, split_cells):
            if loops:
                state[strip, :, lanes] = state[strip, :, lanes] + moved
                continue
            done = state[strip, :, lanes] + moved
            for line in range(ROWS):
                place = pl.ds(lanes.start // STRIP + line, MEMBERS, stride=LINES)
                wide[strip, place, :] = done[:, line * STRIP : (line + 1) * STRIP]
        if not loops:
            message_ref[:, strip * STRIP : (strip + 1) * STRIP] = wide[strip].astype(BF16)
    if loops:
        lax.fori_loop(1, chunks_1, more_cells(ranks_1, table_1, source_of), 0)
        for strip in range(STRIPS):
            for line in range(LINES):
                wide[strip, pl.ds(line, MEMBERS, stride=LINES), :] = state[strip, :, pl.ds(line * STRIP, STRIP)]
            message_ref[:, strip * STRIP : (strip + 1) * STRIP] = wide[strip].astype(BF16)
    return (jnp.maximum(chunks, chunks_1) > 1) | (site_chunks > 1)


def call(kernel, shape, operands, scratch=(), scalars=0, flops=0, moved=1 << 18):
    smem = pl.BlockSpec(memory_space=pltpu.SMEM)
    vmem = pl.BlockSpec(memory_space=pltpu.VMEM)
    return pl.pallas_call(
        kernel,
        out_shape=jax.ShapeDtypeStruct(shape, BF16),
        in_specs=[smem if index < scalars else vmem for index in range(len(operands))],
        out_specs=vmem,
        scratch_shapes=list(scratch),
        compiler_params=pltpu.CompilerParams(vmem_limit_bytes=VMEM_LIMIT),
        cost_estimate=pl.CostEstimate(flops=flops, bytes_accessed=moved, transcendentals=0),
    )(*operands)


MESSAGE = (MEMBERS * LINES, HALF)


def pack(field):
    return call(pack_kernel, MESSAGE, (field,), moved=1 << 20)


def unpack(message):
    return call(unpack_kernel, (LEVELS, CHIPS * ROWS, SPAN_EAST), (message,), moved=1 << 20)


def state_facts(place, datum, noise, point, count):
    smem = pl.BlockSpec(memory_space=pltpu.SMEM)
    vmem = pl.BlockSpec(memory_space=pltpu.VMEM)
    return pl.pallas_call(
        facts_kernel,
        out_shape=jax.ShapeDtypeStruct((FACTS, 2 * SLOTS), BF16),
        in_specs=[smem, vmem, vmem, vmem, smem],
        out_specs=vmem,
        compiler_params=pltpu.CompilerParams(vmem_limit_bytes=VMEM_LIMIT),
    )(place, datum, noise, point, count)


def pick(place, field, own, other):
    scratch = [pltpu.VMEM((2, MEMBERS * LINES, 2 * SLOTS), F32)]
    return call(
        pick_kernel, (PACKET, 4 * SLOTS), (place, field, own, other), scratch, 1, 1 << 27, 1 << 19
    )


def merge(place, own, other, beyond):
    smem = pl.BlockSpec(memory_space=pltpu.SMEM)
    vmem = pl.BlockSpec(memory_space=pltpu.VMEM)
    lanes = (2 * BATCH_LANES, BATCH_LANES + 2 * SLOTS, BATCH_LANES + 2 * SLOTS)
    return pl.pallas_call(
        merge_kernel,
        out_shape=[jax.ShapeDtypeStruct((PACKET, count), BF16) for count in lanes],
        in_specs=[smem, vmem, vmem, vmem],
        out_specs=[vmem, vmem, vmem],
        compiler_params=pltpu.CompilerParams(vmem_limit_bytes=VMEM_LIMIT),
        cost_estimate=pl.CostEstimate(flops=0, bytes_accessed=1 << 18, transcendentals=0),
    )(place, own, other, beyond)


def arrange(field):
    scratch = [pltpu.VMEM((STRIPS, MEMBERS * LINES, STRIP), F32)]
    return call(arrange_kernel, (STRIPS, MEMBERS, LINES * STRIP), (field,), scratch, moved=1 << 20)


def analyse(place, cells, first, here, second):
    scratch = [
        pltpu.VMEM((STRIPS, MEMBERS * LINES, STRIP), F32),
        pltpu.VMEM((STRIPS, MEMBERS, LINES * STRIP), F32),
        pltpu.VMEM((STRIPS, 2 * MEMBERS, LINES * STRIP), BF16),
        pltpu.VMEM((MEMBERS, 2 * BATCH_LANES), F32),
    ]
    return call(
        analysis_kernel, MESSAGE, (place, cells, first, here, second), scratch, 1, 1 << 30, 1 << 20
    )


def swap_cores(block):
    return lax.ppermute(block, "mem", [(i, i ^ 1) for i in range(lax.axis_size("mem"))])


def swap_beyond(block):
    rows, columns = lax.axis_size("mem"), lax.axis_size("tile")
    route = []
    for row in range(0, rows, 2):
        for column in range(columns - 1):
            west, east = (row + 1) * columns + column, row * columns + column + 1
            route += [(west, east), (east, west)]
    return lax.ppermute(block, ("mem", "tile"), route)


def swap_regions(block, start):
    route = []
    for region in range(start, CHIPS - 1, 2):
        for half in range(2):
            one, two = 2 * region + half, 2 * region + 2 + half
            route += [(one, two), (two, one)]
    return lax.ppermute(block, "mem", route)


def on_device(members, datum, noise, point, count):
    row = lax.axis_index("mem")
    column = lax.axis_index("tile")
    half = row % 2
    region = row // 2
    place = jnp.stack(
        [
            row * SPAN_NORTH,
            column * SPAN_EAST,
            half,
            region * ROWS,
            column * SPAN_EAST + half * HALF,
            region % 2,
        ]
    ).astype(jnp.int32)
    message = pack(members[0])
    field = lax.all_to_all(message, "mem", split_axis=0, concat_axis=0, tiled=True)
    facts = state_facts(place, datum, noise, point, count.reshape(2))
    packet = pick(place, field, facts, swap_cores(facts))
    field, packet = lax.optimization_barrier((field, packet))
    beyond = swap_beyond(packet)
    other = swap_cores(packet)
    cells, other, beyond = lax.optimization_barrier((arrange(field), other, beyond))
    here, first, second = merge(place, packet, other, beyond)
    first, second = swap_regions(first, 0), swap_regions(second, 1)
    message = analyse(place, cells, first, here, second)
    message = lax.all_to_all(message, "mem", split_axis=0, concat_axis=0, tiled=True)
    return unpack(message)[None]


def solution(mesh):
    return jax.shard_map(
        on_device,
        mesh=mesh,
        in_specs=(
            P("mem", None, None, "tile"),
            P(None, "mem", "tile", None),
            P(None, "mem", "tile", None),
            P(None, "mem", "tile", None),
            P(None, "mem", "tile"),
        ),
        out_specs=P("mem", None, None, "tile"),
        check_vma=False,
    )
```

```python
import jax
import jax.numpy as jnp
from jax import lax
from jax.experimental import pallas as pl
from jax.experimental.pallas import tpu as pltpu
from jax.sharding import PartitionSpec as P

MEMBERS = 64
LEVELS = 2
SPAN_NORTH = 4
SPAN_EAST = 512
SLOTS = 64
CHIPS = 32
ROWS = 2 * SPAN_NORTH
LINES = LEVELS * ROWS
HALF = SPAN_EAST // 2
STRIP = 128
STRIPS = HALF // STRIP
REACH = 8
CHUNK = 64
SITE_CHUNK = 192
FACTS = 16
PACKET = MEMBERS + FACTS
BATCH_LANES = 4 * SLOTS
F32 = jnp.float32
BF16 = jnp.bfloat16
VMEM_LIMIT = 48 * 1024 * 1024


def split(values):
    high = values.astype(BF16)
    return high, (values - high.astype(F32)).astype(BF16)


def pack_kernel(field_ref, message_ref):
    for group in range(CHIPS // 2):
        upper, lower = (
            field_ref[level, pl.ds(2 * ROWS * group, 2 * ROWS), :].astype(F32) for level in range(LEVELS)
        )
        for chip in range(2):
            rows = slice(chip * ROWS, (chip + 1) * ROWS)
            for half in range(2):
                lanes = slice(half * HALF, (half + 1) * HALF)
                place = (4 * group + 2 * chip + half) * LINES
                message_ref[pl.ds(place, LINES), :] = jnp.concatenate(
                    [upper[rows, lanes], lower[rows, lanes]], axis=0
                ).astype(BF16)


def unpack_kernel(message_ref, field_ref):
    for group in range(CHIPS // 2):
        for half in range(2):
            lanes = pl.ds(half * HALF, HALF)
            first, second = (
                message_ref[pl.ds((4 * group + 2 * chip + half) * LINES, LINES), :].astype(F32)
                for chip in range(2)
            )
            for level in range(LEVELS):
                rows = slice(level * ROWS, (level + 1) * ROWS)
                field_ref[level, pl.ds(2 * ROWS * group, 2 * ROWS), lanes] = jnp.concatenate(
                    [first[rows], second[rows]], axis=0
                ).astype(BF16)


def parts_of(values):
    high = values.astype(BF16).astype(F32)
    rest = values - high
    middle = rest.astype(BF16).astype(F32)
    return [high, middle, rest - middle]


def stack_rows(lines, count):
    shape = (count, lines[0].shape[1])
    rows = lax.broadcasted_iota(jnp.int32, shape, 0)
    block = jnp.zeros(shape, F32)
    for index, line in enumerate(lines):
        block = jnp.where(rows == index, line, block)
    return block


def facts_kernel(place_ref, datum_ref, noise_ref, point_ref, count_ref, facts_ref):
    lane = lax.broadcasted_iota(jnp.int32, (1, 2 * SLOTS), 1)

    def both(ref):
        first = jnp.concatenate([ref[0, 0], ref[0, 0]], axis=1)
        second = jnp.concatenate([ref[1, 0], ref[1, 0]], axis=1)
        return jnp.where(lane < SLOTS, first, second)

    point = both(point_ref)
    count = jnp.where(lane < SLOTS, count_ref[0], count_ref[1])
    col = place_ref[1] + (point & (SPAN_EAST - 1))
    row = place_ref[0] + ((point >> 9) & (SPAN_NORTH - 1))
    live = jnp.where((lane & (SLOTS - 1)) < count, 1.0, 0.0)
    lines = parts_of(both(datum_ref)) + parts_of(both(noise_ref))
    lines += [(col >> 7).astype(F32), (col & 127).astype(F32), row.astype(F32), (point >> 11).astype(F32), live]
    facts_ref[...] = stack_rows(lines, FACTS).astype(BF16)


def pick_kernel(place_ref, field_ref, own_ref, other_ref, packet_ref, scratch):
    own = own_ref[...].astype(F32)
    other = other_ref[...].astype(F32)
    half = place_ref[2]
    first = jnp.where(half == 0, own, other)
    second = jnp.where(half == 0, other, own)
    lane = lax.broadcasted_iota(jnp.int32, first.shape, 1)
    batches = (
        jnp.where(lane < SLOTS, first, pltpu.roll(second, SLOTS, 1)),
        jnp.where(lane < SLOTS, pltpu.roll(first, SLOTS, 1), second),
    )
    place = lax.broadcasted_iota(jnp.int32, (HALF, 2 * SLOTS), 0)
    choosers, lines = [], []
    for facts in batches:
        col = (facts[6:7] * 128.0 + facts[7:8]).astype(jnp.int32) - place_ref[4]
        lines.append((facts[9:10] * ROWS + facts[8:9]).astype(jnp.int32) - place_ref[3])
        choosers.append(jnp.where(place == col, 1.0, 0.0).astype(BF16))
    values = jnp.dot(field_ref[...], jnp.concatenate(choosers, axis=1), preferred_element_type=F32)
    for batch in range(2):
        lanes = pl.ds(batch * 2 * SLOTS, 2 * SLOTS)
        scratch[batch] = values[:, batch * 2 * SLOTS : (batch + 1) * 2 * SLOTS]
        total = jnp.zeros((MEMBERS, 2 * SLOTS), F32)
        for index in range(LINES):
            block = scratch[batch, pl.ds(index, MEMBERS, stride=LINES), :]
            total = total + jnp.where(lines[batch] == index, block, 0.0)
        packet_ref[pl.ds(0, MEMBERS), lanes] = total.astype(BF16)
        packet_ref[pl.ds(MEMBERS, FACTS), lanes] = batches[batch].astype(BF16)


def merge_kernel(place_ref, own_ref, other_ref, beyond_ref, here_ref, first_ref, second_ref):
    lane = lax.broadcasted_iota(jnp.int32, (PACKET, 2 * SLOTS), 1)
    odd = place_ref[5]
    for batch in range(2):
        lanes = pl.ds(batch * 2 * SLOTS, 2 * SLOTS)
        members = pl.ds(0, MEMBERS)
        here = jnp.concatenate(
            [own_ref[members, lanes] + other_ref[members, lanes], own_ref[pl.ds(MEMBERS, FACTS), lanes]],
            axis=0,
        ).astype(F32)
        beyond = beyond_ref[:, lanes].astype(F32)
        upper = jnp.where(lane < SLOTS, here, pltpu.roll(beyond, SLOTS, 1))
        lower = jnp.where(lane < SLOTS, pltpu.roll(here, SLOTS, 1), beyond)
        start = batch * BATCH_LANES
        here_ref[:, pl.ds(start, 2 * SLOTS)] = upper.astype(BF16)
        here_ref[:, pl.ds(start + 2 * SLOTS, 2 * SLOTS)] = lower.astype(BF16)
        if batch == 0:
            for ref in (first_ref, second_ref):
                ref[:, pl.ds(0, 2 * SLOTS)] = upper.astype(BF16)
                ref[:, pl.ds(2 * SLOTS, 2 * SLOTS)] = lower.astype(BF16)
        else:
            first_ref[:, pl.ds(start, 2 * SLOTS)] = jnp.where(odd == 0, lower, upper).astype(BF16)
            second_ref[:, pl.ds(start, 2 * SLOTS)] = jnp.where(odd == 0, upper, lower).astype(BF16)


def weights_of(columns, datum, noise, live):
    mean = jnp.sum(columns, axis=0, keepdims=True) * (1.0 / MEMBERS)
    pert = columns - mean
    variance = jnp.sum(pert * pert, axis=0, keepdims=True) / (MEMBERS - 1)
    denominator = jnp.where(live > 0.0, variance + noise, 1.0)
    factor = 1.0 / (1.0 + jnp.sqrt(noise / denominator))
    return pert, live * (datum - mean) / denominator, live * factor / denominator


def positions(masks):
    rows, lanes = masks.shape
    before = lax.broadcasted_iota(jnp.int32, (128, 128), 0)
    after = lax.broadcasted_iota(jnp.int32, (128, 128), 1)
    triangle = jnp.where(before < after, 1.0, 0.0).astype(BF16)
    total = jnp.zeros((rows, 1), F32)
    parts = []
    for start in range(0, lanes, 128):
        block = masks[:, start : start + 128]
        rank = jnp.dot(block.astype(BF16), triangle, preferred_element_type=F32) + total
        parts.append(jnp.where(block > 0.0, rank, -1.0))
        total = total + jnp.sum(block, axis=1, keepdims=True)
    return jnp.concatenate(parts, axis=1), total


def taper(square):
    inverse = lax.rsqrt(jnp.maximum(square, 1.0))
    distance = square * inverse
    inside = ((distance * (-0.25 / 1024.0) + 0.5 / 256.0) * distance + 0.625 / 64.0) * distance
    inside = (inside - 5.0 / 48.0) * square + 1.0
    left = jnp.maximum(8.0 - distance, 0.0)
    left = left * left
    outside = (distance * (0.125 / 1536.0) + 1.0 / 1536.0) * distance - 1.0 / 1536.0
    outside = outside * inverse * (left * left)
    return jnp.where(square <= 16.0, inside, outside)


def table_of(pert, mean_weight, pert_weight, row, col, level):
    high, low = split(pert)
    tail = [row.astype(F32), (col & ~127).astype(F32), (col & 127).astype(F32), level]
    for weight in (mean_weight, pert_weight):
        weight_high, weight_low = split(weight)
        tail += [weight_high.astype(F32), weight_low.astype(F32)]
    return jnp.concatenate([high, low, stack_rows(tail, 16).astype(BF16)], axis=0)


def chosen_records(ranks, bases, counts, table):
    parts = []
    for index, (base, count) in enumerate(zip(bases, counts)):
        place = lax.broadcasted_iota(jnp.int32, (count, 1), 0).astype(F32) + base
        parts.append(jnp.where(ranks[index : index + 1] == place, 1.0, 0.0).astype(BF16))
    chooser = jnp.concatenate(parts, axis=0)
    return lax.dot_general(chooser, table, (((1,), (1,)), ((), ())), preferred_element_type=F32)


def open_records(records):
    pert = records[:, : 2 * MEMBERS].astype(BF16)
    tail = records[:, 2 * MEMBERS :]
    row = tail[:, 0:1]
    col = tail[:, 1:2] + tail[:, 2:3]
    level = tail[:, 3:4]
    mean_weight = tail[:, 4:5] + tail[:, 5:6]
    pert_weight = tail[:, 6:7] + tail[:, 7:8]
    step = mean_weight - pert_weight * (records[:, :MEMBERS] + records[:, MEMBERS : 2 * MEMBERS])
    return pert, row, col, level, step * (1.0 / (MEMBERS - 1))


def halves(gain):
    high, low = split(gain)
    return jnp.concatenate([high, high, low], axis=0)


def advance(step, gain):
    high, low = split(step)
    return lax.dot_general(
        jnp.concatenate([high, low, high], axis=0),
        gain,
        (((0,), (0,)), ((), ())),
        preferred_element_type=F32,
    )


def region_step(records, strip, matched):
    pert, row, col, level, step = open_records(records)
    lane = lax.broadcasted_iota(jnp.int32, (1, STRIP), 1).astype(F32) + strip * STRIP
    across = col - lane
    across = across * across
    tile = jnp.floor(row * (1.0 / SPAN_NORTH))
    tapers = []
    for line in range(ROWS):
        down = row - float(line)
        tapers.append(taper(across + down * down))
    for target in range(LEVELS):
        factor = jnp.where(level == target, 1.0, 0.5)
        factors = [
            jnp.where(jnp.abs(tile - part) <= 1.0, factor, 0.0) for part in range(ROWS // SPAN_NORTH)
        ]
        weight = jnp.concatenate(
            [tapers[line] * factors[line // SPAN_NORTH] for line in range(ROWS)], axis=1
        )
        lanes = pl.ds(target * ROWS * STRIP, ROWS * STRIP)
        cells = matched(strip, lanes)
        if cells.shape[0] > 2 * MEMBERS:
            three = jnp.concatenate([pert, pert[:, :MEMBERS]], axis=1)
            covariance = jnp.dot(three, cells, preferred_element_type=F32)
        else:
            covariance = jnp.dot(pert, cells, preferred_element_type=F32)
        yield lanes, advance(step, halves(weight * covariance))


def chunks_of(total, size):
    return (jnp.max(total).astype(jnp.int32) + (size - 1)) // size


def rows_of(cats, rows, batch):
    parts = []
    for index, cat in enumerate(cats):
        count = 2 * SLOTS if batch == 1 and index != 1 else BATCH_LANES
        parts.append(cat[rows, pl.ds(batch * BATCH_LANES, count)])
    return jnp.concatenate(parts, axis=1)


def facts_of(cats, batch, place_ref):
    facts = rows_of(cats, pl.ds(MEMBERS, FACTS), batch).astype(F32)
    datum = facts[0:1] + facts[1:2] + facts[2:3]
    noise = facts[3:4] + facts[4:5] + facts[5:6]
    col = (facts[6:7] * 128.0 + facts[7:8]).astype(jnp.int32) - place_ref[4]
    row = facts[8:9].astype(jnp.int32) - place_ref[3]
    return datum, noise, col, row, facts[9:10], facts[10:11]


def masks_of(col, row, live):
    masks = []
    for strip in range(STRIPS):
        west = strip * STRIP - REACH
        inside = (col > west) & (col < west + STRIP + 2 * REACH - 1)
        inside = inside & (row >= -SPAN_NORTH) & (row < ROWS + SPAN_NORTH)
        masks.append(jnp.where(inside, live, 0.0))
    inside = (col > -2 * REACH) & (col < HALF + 2 * REACH - 1)
    masks.append(jnp.where(inside, live, 0.0))
    return stack_rows(masks, 8)


def arrange_kernel(field_ref, cells_ref, wide):
    for strip in range(STRIPS):
        wide[strip] = field_ref[:, strip * STRIP : (strip + 1) * STRIP].astype(F32)
    for strip in range(STRIPS):
        for line in range(LINES):
            piece = wide[strip, pl.ds(line, MEMBERS, stride=LINES), :]
            cells_ref[strip, :, pl.ds(line * STRIP, STRIP)] = piece.astype(BF16)


def analysis_kernel(place_ref, cells_ref, next_ref, here_ref, last_ref, message_ref, *scratch):
    refs = (place_ref, cells_ref, (next_ref, here_ref, last_ref), message_ref, *scratch)
    more = analysis(False, *refs)

    @pl.when(more)
    def _():
        analysis(True, *refs)


def analysis(loops, place_ref, cells, cats, message_ref, wide, state, source, site_state):
    sizes = [CHUNK] * STRIPS
    pieces = [slice(strip * CHUNK, (strip + 1) * CHUNK) for strip in range(STRIPS)]
    members = pl.ds(0, MEMBERS)

    datum, noise, col, row, level, live = facts_of(cats, 0, place_ref)
    datum_1, noise_1, col_1, row_1, level_1, live_1 = facts_of(cats, 1, place_ref)
    ranks, total = positions(masks_of(col, row, live))
    ranks_1, total_1 = positions(masks_of(col_1, row_1, live_1))
    chunks = chunks_of(total[:STRIPS], CHUNK)
    chunks_1 = chunks_of(total_1[:STRIPS], CHUNK)
    site_chunks = chunks_of(total[STRIPS : STRIPS + 1], SITE_CHUNK)

    first = rows_of(cats, members, 0).astype(F32)
    pert, mean_weight, pert_weight = weights_of(first, datum, noise, live)
    table = table_of(pert, mean_weight, pert_weight, row, col, level)
    records = chosen_records(ranks, [0.0] * (STRIPS + 1), sizes + [SITE_CHUNK], table)

    sites = rows_of(cats, members, 1)
    site_row = row_1.astype(F32)
    site_col = col_1.astype(F32)
    site_tile = (row_1 >> 2).astype(F32)

    def site_step(records):
        obs, obs_row, obs_col, obs_level, step = open_records(records)
        down = obs_row - site_row
        across = obs_col - site_col
        weight = taper(down * down + across * across)
        weight = weight * jnp.where(obs_level == level_1, 1.0, 0.5)
        obs_tile = jnp.floor(obs_row * (1.0 / SPAN_NORTH))
        weight = jnp.where(jnp.abs(obs_tile - site_tile) <= 1.0, weight, 0.0)
        covariance = jnp.dot(obs, jnp.concatenate([sites, sites], axis=0), preferred_element_type=F32)
        return advance(step, halves(weight * covariance))

    after = sites.astype(F32) + site_step(records[STRIPS * CHUNK :])

    def more_sites(index, carry):
        base = (index * SITE_CHUNK).astype(F32)
        more = chosen_records(ranks[STRIPS : STRIPS + 1], [base], [SITE_CHUNK], table)
        site_state[...] = site_state[...] + site_step(more)
        return carry

    if loops:
        site_state[...] = after
        lax.fori_loop(1, site_chunks, more_sites, 0)
        after = site_state[...]

    def more_cells(ranks, table, matched):
        def one(index, carry):
            base = (index * CHUNK).astype(F32)
            more = chosen_records(ranks, [base] * STRIPS, sizes, table)
            for strip in range(STRIPS):
                for lanes, moved in region_step(more[pieces[strip]], strip, matched):
                    state[strip, :, lanes] = state[strip, :, lanes] + moved
            return carry

        return one

    pert, mean_weight, pert_weight = weights_of(after, datum_1, noise_1, live_1)
    table_1 = table_of(pert, mean_weight, pert_weight, row_1, col_1, level_1)
    records_1 = chosen_records(ranks_1, [0.0] * STRIPS, sizes, table_1)

    def cells_of(strip, lanes):
        once = cells[strip, :, lanes]
        return jnp.concatenate([once, once], axis=0)

    for strip in range(STRIPS):
        for lanes, moved in region_step(records[pieces[strip]], strip, cells_of):
            state[strip, :, lanes] = cells[strip, :, lanes].astype(F32) + moved
    if loops:
        lax.fori_loop(1, chunks, more_cells(ranks, table, cells_of), 0)


    def split_cells(strip, lanes):
        high, low = split(state[strip, :, lanes])
        if loops:
            source[strip, :MEMBERS, lanes] = high
            source[strip, MEMBERS:, lanes] = low
        return jnp.concatenate([high, high, low], axis=0)

    def source_of(strip, lanes):
        high = source[strip, :MEMBERS, lanes]
        return jnp.concatenate([high, high, source[strip, MEMBERS:, lanes]], axis=0)

    for strip in range(STRIPS):
        for lanes, moved in region_step(records_1[pieces[strip]], strip, split_cells):
            if loops:
                state[strip, :, lanes] = state[strip, :, lanes] + moved
                continue
            done = state[strip, :, lanes] + moved
            for line in range(ROWS):
                place = pl.ds(lanes.start // STRIP + line, MEMBERS, stride=LINES)
                wide[strip, place, :] = done[:, line * STRIP : (line + 1) * STRIP]
        if not loops:
            message_ref[:, strip * STRIP : (strip + 1) * STRIP] = wide[strip].astype(BF16)
    if loops:
        lax.fori_loop(1, chunks_1, more_cells(ranks_1, table_1, source_of), 0)
        for strip in range(STRIPS):
            for line in range(LINES):
                wide[strip, pl.ds(line, MEMBERS, stride=LINES), :] = state[strip, :, pl.ds(line * STRIP, STRIP)]
            message_ref[:, strip * STRIP : (strip + 1) * STRIP] = wide[strip].astype(BF16)
    return (jnp.maximum(chunks, chunks_1) > 1) | (site_chunks > 1)


def call(kernel, shape, operands, scratch=(), scalars=0, flops=0, moved=1 << 18):
    smem = pl.BlockSpec(memory_space=pltpu.SMEM)
    vmem = pl.BlockSpec(memory_space=pltpu.VMEM)
    return pl.pallas_call(
        kernel,
        out_shape=jax.ShapeDtypeStruct(shape, BF16),
        in_specs=[smem if index < scalars else vmem for index in range(len(operands))],
        out_specs=vmem,
        scratch_shapes=list(scratch),
        compiler_params=pltpu.CompilerParams(vmem_limit_bytes=VMEM_LIMIT),
        cost_estimate=pl.CostEstimate(flops=flops, bytes_accessed=moved, transcendentals=0),
    )(*operands)


MESSAGE = (MEMBERS * LINES, HALF)


def pack(field):
    return call(pack_kernel, MESSAGE, (field,), moved=1 << 20)


def unpack(message):
    return call(unpack_kernel, (LEVELS, CHIPS * ROWS, SPAN_EAST), (message,), moved=1 << 20)


def state_facts(place, datum, noise, point, count):
    smem = pl.BlockSpec(memory_space=pltpu.SMEM)
    vmem = pl.BlockSpec(memory_space=pltpu.VMEM)
    return pl.pallas_call(
        facts_kernel,
        out_shape=jax.ShapeDtypeStruct((FACTS, 2 * SLOTS), BF16),
        in_specs=[smem, vmem, vmem, vmem, smem],
        out_specs=vmem,
        compiler_params=pltpu.CompilerParams(vmem_limit_bytes=VMEM_LIMIT),
    )(place, datum, noise, point, count)


def pick(place, field, own, other):
    scratch = [pltpu.VMEM((2, MEMBERS * LINES, 2 * SLOTS), F32)]
    return call(
        pick_kernel, (PACKET, 4 * SLOTS), (place, field, own, other), scratch, 1, 1 << 27, 1 << 19
    )


def merge(place, own, other, beyond):
    smem = pl.BlockSpec(memory_space=pltpu.SMEM)
    vmem = pl.BlockSpec(memory_space=pltpu.VMEM)
    lanes = (2 * BATCH_LANES, BATCH_LANES + 2 * SLOTS, BATCH_LANES + 2 * SLOTS)
    return pl.pallas_call(
        merge_kernel,
        out_shape=[jax.ShapeDtypeStruct((PACKET, count), BF16) for count in lanes],
        in_specs=[smem, vmem, vmem, vmem],
        out_specs=[vmem, vmem, vmem],
        compiler_params=pltpu.CompilerParams(vmem_limit_bytes=VMEM_LIMIT),
        cost_estimate=pl.CostEstimate(flops=0, bytes_accessed=1 << 18, transcendentals=0),
    )(place, own, other, beyond)


def arrange(field):
    scratch = [pltpu.VMEM((STRIPS, MEMBERS * LINES, STRIP), F32)]
    return call(arrange_kernel, (STRIPS, MEMBERS, LINES * STRIP), (field,), scratch, moved=1 << 20)


def analyse(place, cells, first, here, second):
    scratch = [
        pltpu.VMEM((STRIPS, MEMBERS * LINES, STRIP), F32),
        pltpu.VMEM((STRIPS, MEMBERS, LINES * STRIP), F32),
        pltpu.VMEM((STRIPS, 2 * MEMBERS, LINES * STRIP), BF16),
        pltpu.VMEM((MEMBERS, 2 * BATCH_LANES), F32),
    ]
    return call(
        analysis_kernel, MESSAGE, (place, cells, first, here, second), scratch, 1, 1 << 30, 1 << 20
    )


def swap_cores(block):
    return lax.ppermute(block, "mem", [(i, i ^ 1) for i in range(lax.axis_size("mem"))])


def swap_beyond(block):
    rows, columns = lax.axis_size("mem"), lax.axis_size("tile")
    route = []
    for row in range(0, rows, 2):
        for column in range(columns - 1):
            west, east = (row + 1) * columns + column, row * columns + column + 1
            route += [(west, east), (east, west)]
    return lax.ppermute(block, ("mem", "tile"), route)


def swap_regions(block, start):
    route = []
    for region in range(start, CHIPS - 1, 2):
        for half in range(2):
            one, two = 2 * region + half, 2 * region + 2 + half
            route += [(one, two), (two, one)]
    return lax.ppermute(block, "mem", route)


def on_device(members, datum, noise, point, count):
    row = lax.axis_index("mem")
    column = lax.axis_index("tile")
    half = row % 2
    region = row // 2
    place = jnp.stack(
        [
            row * SPAN_NORTH,
            column * SPAN_EAST,
            half,
            region * ROWS,
            column * SPAN_EAST + half * HALF,
            region % 2,
        ]
    ).astype(jnp.int32)
    message = pack(members[0])
    field = lax.all_to_all(message, "mem", split_axis=0, concat_axis=0, tiled=True)
    facts = state_facts(place, datum, noise, point, count.reshape(2))
    packet = pick(place, field, facts, swap_cores(facts))
    field, packet = lax.optimization_barrier((field, packet))
    beyond = swap_beyond(packet)
    other = swap_cores(packet)
    cells, other, beyond = lax.optimization_barrier((arrange(field), other, beyond))
    here, first, second = merge(place, packet, other, beyond)
    first, second = swap_regions(first, 0), swap_regions(second, 1)
    message = analyse(place, cells, first, here, second)
    message = lax.all_to_all(message, "mem", split_axis=0, concat_axis=0, tiled=True)
    return unpack(message)[None]


def solution(mesh):
    return jax.shard_map(
        on_device,
        mesh=mesh,
        in_specs=(
            P("mem", None, None, "tile"),
            P(None, "mem", "tile", None),
            P(None, "mem", "tile", None),
            P(None, "mem", "tile", None),
            P(None, "mem", "tile"),
        ),
        out_specs=P("mem", None, None, "tile"),
        check_vma=False,
    )
```

```python
import jax
import jax.numpy as jnp
from jax import lax
from jax.experimental import pallas as pl
from jax.experimental.pallas import tpu as pltpu
from jax.sharding import PartitionSpec as P

MEMBERS = 64
LEVELS = 2
SPAN_NORTH = 4
SPAN_EAST = 512
SLOTS = 64
CHIPS = 32
ROWS = 2 * SPAN_NORTH
LINES = LEVELS * ROWS
HALF = SPAN_EAST // 2
STRIP = 128
STRIPS = HALF // STRIP
REACH = 8
CHUNK = 64
SITE_CHUNK = 192
FACTS = 16
PACKET = MEMBERS + FACTS
BATCH_LANES = 4 * SLOTS
F32 = jnp.float32
BF16 = jnp.bfloat16
VMEM_LIMIT = 48 * 1024 * 1024


def split(values):
    high = values.astype(BF16)
    return high, (values - high.astype(F32)).astype(BF16)


def pack_kernel(field_ref, message_ref):
    for group in range(CHIPS // 2):
        upper, lower = (
            field_ref[level, pl.ds(2 * ROWS * group, 2 * ROWS), :].astype(F32) for level in range(LEVELS)
        )
        for chip in range(2):
            rows = slice(chip * ROWS, (chip + 1) * ROWS)
            for half in range(2):
                lanes = slice(half * HALF, (half + 1) * HALF)
                place = (4 * group + 2 * chip + half) * LINES
                message_ref[pl.ds(place, LINES), :] = jnp.concatenate(
                    [upper[rows, lanes], lower[rows, lanes]], axis=0
                ).astype(BF16)


def unpack_kernel(message_ref, field_ref):
    for group in range(CHIPS // 2):
        for half in range(2):
            lanes = pl.ds(half * HALF, HALF)
            first, second = (
                message_ref[pl.ds((4 * group + 2 * chip + half) * LINES, LINES), :].astype(F32)
                for chip in range(2)
            )
            for level in range(LEVELS):
                rows = slice(level * ROWS, (level + 1) * ROWS)
                field_ref[level, pl.ds(2 * ROWS * group, 2 * ROWS), lanes] = jnp.concatenate(
                    [first[rows], second[rows]], axis=0
                ).astype(BF16)


def parts_of(values):
    high = values.astype(BF16).astype(F32)
    rest = values - high
    middle = rest.astype(BF16).astype(F32)
    return [high, middle, rest - middle]


def stack_rows(lines, count):
    shape = (count, lines[0].shape[1])
    rows = lax.broadcasted_iota(jnp.int32, shape, 0)
    block = jnp.zeros(shape, F32)
    for index, line in enumerate(lines):
        block = jnp.where(rows == index, line, block)
    return block


def facts_kernel(place_ref, datum_ref, noise_ref, point_ref, count_ref, facts_ref):
    lane = lax.broadcasted_iota(jnp.int32, (1, 2 * SLOTS), 1)

    def both(ref):
        first = jnp.concatenate([ref[0, 0], ref[0, 0]], axis=1)
        second = jnp.concatenate([ref[1, 0], ref[1, 0]], axis=1)
        return jnp.where(lane < SLOTS, first, second)

    point = both(point_ref)
    count = jnp.where(lane < SLOTS, count_ref[0], count_ref[1])
    col = place_ref[1] + (point & (SPAN_EAST - 1))
    row = place_ref[0] + ((point >> 9) & (SPAN_NORTH - 1))
    live = jnp.where((lane & (SLOTS - 1)) < count, 1.0, 0.0)
    lines = parts_of(both(datum_ref)) + parts_of(both(noise_ref))
    lines += [(col >> 7).astype(F32), (col & 127).astype(F32), row.astype(F32), (point >> 11).astype(F32), live]
    facts_ref[...] = stack_rows(lines, FACTS).astype(BF16)


def choose_kernel(place_ref, own_ref, other_ref, chooser_ref, facts_ref):
    own = own_ref[...].astype(F32)
    other = other_ref[...].astype(F32)
    half = place_ref[2]
    first = jnp.where(half == 0, own, other)
    second = jnp.where(half == 0, other, own)
    lane = lax.broadcasted_iota(jnp.int32, first.shape, 1)
    batches = (
        jnp.where(lane < SLOTS, first, pltpu.roll(second, SLOTS, 1)),
        jnp.where(lane < SLOTS, pltpu.roll(first, SLOTS, 1), second),
    )
    place = lax.broadcasted_iota(jnp.int32, (HALF, 2 * SLOTS), 0)
    for batch, facts in enumerate(batches):
        lanes = pl.ds(batch * 2 * SLOTS, 2 * SLOTS)
        col = (facts[6:7] * 128.0 + facts[7:8]).astype(jnp.int32) - place_ref[4]
        chooser_ref[:, lanes] = jnp.where(place == col, 1.0, 0.0).astype(BF16)
        facts_ref[:, lanes] = facts.astype(BF16)


def pick_kernel(place_ref, field_ref, chooser_ref, facts_ref, packet_ref, scratch):
    facts = facts_ref[...].astype(F32)
    line = (facts[9:10] * ROWS + facts[8:9]).astype(jnp.int32) - place_ref[3]
    values = jnp.dot(field_ref[...], chooser_ref[...], preferred_element_type=F32)
    for batch in range(2):
        part = slice(batch * 2 * SLOTS, (batch + 1) * 2 * SLOTS)
        scratch[batch] = values[:, part]
        total = jnp.zeros((MEMBERS, 2 * SLOTS), F32)
        for index in range(LINES):
            block = scratch[batch, pl.ds(index, MEMBERS, stride=LINES), :]
            total = total + jnp.where(line[:, part] == index, block, 0.0)
        packet_ref[pl.ds(0, MEMBERS), pl.ds(batch * 2 * SLOTS, 2 * SLOTS)] = total.astype(BF16)
    packet_ref[pl.ds(MEMBERS, FACTS), :] = facts_ref[...]


def merge_kernel(place_ref, own_ref, other_ref, beyond_ref, here_ref, first_ref, second_ref):
    lane = lax.broadcasted_iota(jnp.int32, (PACKET, 2 * SLOTS), 1)
    odd = place_ref[5]
    for batch in range(2):
        lanes = pl.ds(batch * 2 * SLOTS, 2 * SLOTS)
        members = pl.ds(0, MEMBERS)
        here = jnp.concatenate(
            [own_ref[members, lanes] + other_ref[members, lanes], own_ref[pl.ds(MEMBERS, FACTS), lanes]],
            axis=0,
        ).astype(F32)
        beyond = beyond_ref[:, lanes].astype(F32)
        upper = jnp.where(lane < SLOTS, here, pltpu.roll(beyond, SLOTS, 1))
        lower = jnp.where(lane < SLOTS, pltpu.roll(here, SLOTS, 1), beyond)
        start = batch * BATCH_LANES
        here_ref[:, pl.ds(start, 2 * SLOTS)] = upper.astype(BF16)
        here_ref[:, pl.ds(start + 2 * SLOTS, 2 * SLOTS)] = lower.astype(BF16)
        if batch == 0:
            for ref in (first_ref, second_ref):
                ref[:, pl.ds(0, 2 * SLOTS)] = upper.astype(BF16)
                ref[:, pl.ds(2 * SLOTS, 2 * SLOTS)] = lower.astype(BF16)
        else:
            first_ref[:, pl.ds(start, 2 * SLOTS)] = jnp.where(odd == 0, lower, upper).astype(BF16)
            second_ref[:, pl.ds(start, 2 * SLOTS)] = jnp.where(odd == 0, upper, lower).astype(BF16)


def weights_of(columns, datum, noise, live):
    mean = jnp.sum(columns, axis=0, keepdims=True) * (1.0 / MEMBERS)
    pert = columns - mean
    variance = jnp.sum(pert * pert, axis=0, keepdims=True) / (MEMBERS - 1)
    denominator = jnp.where(live > 0.0, variance + noise, 1.0)
    factor = 1.0 / (1.0 + jnp.sqrt(noise / denominator))
    return pert, live * (datum - mean) / denominator, live * factor / denominator


def positions(masks):
    rows, lanes = masks.shape
    before = lax.broadcasted_iota(jnp.int32, (128, 128), 0)
    after = lax.broadcasted_iota(jnp.int32, (128, 128), 1)
    triangle = jnp.where(before < after, 1.0, 0.0).astype(BF16)
    total = jnp.zeros((rows, 1), F32)
    parts = []
    for start in range(0, lanes, 128):
        block = masks[:, start : start + 128]
        rank = jnp.dot(block.astype(BF16), triangle, preferred_element_type=F32) + total
        parts.append(jnp.where(block > 0.0, rank, -1.0))
        total = total + jnp.sum(block, axis=1, keepdims=True)
    return jnp.concatenate(parts, axis=1), total


def taper(square):
    inverse = lax.rsqrt(jnp.maximum(square, 1.0))
    distance = square * inverse
    inside = ((distance * (-0.25 / 1024.0) + 0.5 / 256.0) * distance + 0.625 / 64.0) * distance
    inside = (inside - 5.0 / 48.0) * square + 1.0
    left = jnp.maximum(8.0 - distance, 0.0)
    left = left * left
    outside = (distance * (0.125 / 1536.0) + 1.0 / 1536.0) * distance - 1.0 / 1536.0
    outside = outside * inverse * (left * left)
    return jnp.where(square <= 16.0, inside, outside)


def table_of(pert, mean_weight, pert_weight, row, col, level):
    high, low = split(pert)
    tail = [row.astype(F32), (col & ~127).astype(F32), (col & 127).astype(F32), level]
    for weight in (mean_weight, pert_weight):
        weight_high, weight_low = split(weight)
        tail += [weight_high.astype(F32), weight_low.astype(F32)]
    return jnp.concatenate([high, low, stack_rows(tail, 16).astype(BF16)], axis=0)


def chosen_records(ranks, bases, counts, table):
    parts = []
    for index, (base, count) in enumerate(zip(bases, counts)):
        place = lax.broadcasted_iota(jnp.int32, (count, 1), 0).astype(F32) + base
        parts.append(jnp.where(ranks[index : index + 1] == place, 1.0, 0.0).astype(BF16))
    chooser = jnp.concatenate(parts, axis=0)
    return lax.dot_general(chooser, table, (((1,), (1,)), ((), ())), preferred_element_type=F32)


def open_records(records):
    pert = records[:, : 2 * MEMBERS].astype(BF16)
    tail = records[:, 2 * MEMBERS :]
    row = tail[:, 0:1]
    col = tail[:, 1:2] + tail[:, 2:3]
    level = tail[:, 3:4]
    mean_weight = tail[:, 4:5] + tail[:, 5:6]
    pert_weight = tail[:, 6:7] + tail[:, 7:8]
    step = mean_weight - pert_weight * (records[:, :MEMBERS] + records[:, MEMBERS : 2 * MEMBERS])
    return pert, row, col, level, step * (1.0 / (MEMBERS - 1))


def halves(gain):
    high, low = split(gain)
    return jnp.concatenate([high, high, low], axis=0)


def advance(step, gain):
    high, low = split(step)
    return lax.dot_general(
        jnp.concatenate([high, low, high], axis=0),
        gain,
        (((0,), (0,)), ((), ())),
        preferred_element_type=F32,
    )


def region_step(records, strip, matched):
    pert, row, col, level, step = open_records(records)
    lane = lax.broadcasted_iota(jnp.int32, (1, STRIP), 1).astype(F32) + strip * STRIP
    across = col - lane
    across = across * across
    tile = jnp.floor(row * (1.0 / SPAN_NORTH))
    tapers = []
    for line in range(ROWS):
        down = row - float(line)
        tapers.append(taper(across + down * down))
    for target in range(LEVELS):
        factor = jnp.where(level == target, 1.0, 0.5)
        factors = [
            jnp.where(jnp.abs(tile - part) <= 1.0, factor, 0.0) for part in range(ROWS // SPAN_NORTH)
        ]
        weight = jnp.concatenate(
            [tapers[line] * factors[line // SPAN_NORTH] for line in range(ROWS)], axis=1
        )
        lanes = pl.ds(target * ROWS * STRIP, ROWS * STRIP)
        cells = matched(strip, lanes)
        if cells.shape[0] > 2 * MEMBERS:
            three = jnp.concatenate([pert, pert[:, :MEMBERS]], axis=1)
            covariance = jnp.dot(three, cells, preferred_element_type=F32)
        else:
            covariance = jnp.dot(pert, cells, preferred_element_type=F32)
        yield lanes, advance(step, halves(weight * covariance))


def chunks_of(total, size):
    return (jnp.max(total).astype(jnp.int32) + (size - 1)) // size


def rows_of(cats, rows, batch):
    parts = []
    for index, cat in enumerate(cats):
        count = 2 * SLOTS if batch == 1 and index != 1 else BATCH_LANES
        parts.append(cat[rows, pl.ds(batch * BATCH_LANES, count)])
    return jnp.concatenate(parts, axis=1)


def facts_of(cats, batch, place_ref):
    facts = rows_of(cats, pl.ds(MEMBERS, FACTS), batch).astype(F32)
    datum = facts[0:1] + facts[1:2] + facts[2:3]
    noise = facts[3:4] + facts[4:5] + facts[5:6]
    col = (facts[6:7] * 128.0 + facts[7:8]).astype(jnp.int32) - place_ref[4]
    row = facts[8:9].astype(jnp.int32) - place_ref[3]
    return datum, noise, col, row, facts[9:10], facts[10:11]


def masks_of(col, row, live):
    masks = []
    for strip in range(STRIPS):
        west = strip * STRIP - REACH
        inside = (col > west) & (col < west + STRIP + 2 * REACH - 1)
        inside = inside & (row >= -SPAN_NORTH) & (row < ROWS + SPAN_NORTH)
        masks.append(jnp.where(inside, live, 0.0))
    inside = (col > -2 * REACH) & (col < HALF + 2 * REACH - 1)
    masks.append(jnp.where(inside, live, 0.0))
    return stack_rows(masks, 8)


def arrange_kernel(field_ref, cells_ref, wide):
    for strip in range(STRIPS):
        wide[strip] = field_ref[:, strip * STRIP : (strip + 1) * STRIP].astype(F32)
    for strip in range(STRIPS):
        for line in range(LINES):
            piece = wide[strip, pl.ds(line, MEMBERS, stride=LINES), :]
            cells_ref[strip, :, pl.ds(line * STRIP, STRIP)] = piece.astype(BF16)


def analysis_kernel(place_ref, cells_ref, next_ref, here_ref, last_ref, message_ref, *scratch):
    refs = (place_ref, cells_ref, (next_ref, here_ref, last_ref), message_ref, *scratch)
    more = analysis(False, *refs)

    @pl.when(more)
    def _():
        analysis(True, *refs)


def analysis(loops, place_ref, cells, cats, message_ref, wide, state, source, site_state):
    sizes = [CHUNK] * STRIPS
    pieces = [slice(strip * CHUNK, (strip + 1) * CHUNK) for strip in range(STRIPS)]
    members = pl.ds(0, MEMBERS)

    datum, noise, col, row, level, live = facts_of(cats, 0, place_ref)
    datum_1, noise_1, col_1, row_1, level_1, live_1 = facts_of(cats, 1, place_ref)
    ranks, total = positions(masks_of(col, row, live))
    ranks_1, total_1 = positions(masks_of(col_1, row_1, live_1))
    chunks = chunks_of(total[:STRIPS], CHUNK)
    chunks_1 = chunks_of(total_1[:STRIPS], CHUNK)
    site_chunks = chunks_of(total[STRIPS : STRIPS + 1], SITE_CHUNK)

    first = rows_of(cats, members, 0).astype(F32)
    pert, mean_weight, pert_weight = weights_of(first, datum, noise, live)
    table = table_of(pert, mean_weight, pert_weight, row, col, level)
    records = chosen_records(ranks, [0.0] * (STRIPS + 1), sizes + [SITE_CHUNK], table)

    sites = rows_of(cats, members, 1)
    site_row = row_1.astype(F32)
    site_col = col_1.astype(F32)
    site_tile = (row_1 >> 2).astype(F32)

    def site_step(records):
        obs, obs_row, obs_col, obs_level, step = open_records(records)
        down = obs_row - site_row
        across = obs_col - site_col
        weight = taper(down * down + across * across)
        weight = weight * jnp.where(obs_level == level_1, 1.0, 0.5)
        obs_tile = jnp.floor(obs_row * (1.0 / SPAN_NORTH))
        weight = jnp.where(jnp.abs(obs_tile - site_tile) <= 1.0, weight, 0.0)
        covariance = jnp.dot(obs, jnp.concatenate([sites, sites], axis=0), preferred_element_type=F32)
        return advance(step, halves(weight * covariance))

    after = sites.astype(F32) + site_step(records[STRIPS * CHUNK :])

    def more_sites(index, carry):
        base = (index * SITE_CHUNK).astype(F32)
        more = chosen_records(ranks[STRIPS : STRIPS + 1], [base], [SITE_CHUNK], table)
        site_state[...] = site_state[...] + site_step(more)
        return carry

    if loops:
        site_state[...] = after
        lax.fori_loop(1, site_chunks, more_sites, 0)
        after = site_state[...]

    def more_cells(ranks, table, matched):
        def one(index, carry):
            base = (index * CHUNK).astype(F32)
            more = chosen_records(ranks, [base] * STRIPS, sizes, table)
            for strip in range(STRIPS):
                for lanes, moved in region_step(more[pieces[strip]], strip, matched):
                    state[strip, :, lanes] = state[strip, :, lanes] + moved
            return carry

        return one

    pert, mean_weight, pert_weight = weights_of(after, datum_1, noise_1, live_1)
    table_1 = table_of(pert, mean_weight, pert_weight, row_1, col_1, level_1)
    records_1 = chosen_records(ranks_1, [0.0] * STRIPS, sizes, table_1)

    def cells_of(strip, lanes):
        once = cells[strip, :, lanes]
        return jnp.concatenate([once, once], axis=0)

    for strip in range(STRIPS):
        for lanes, moved in region_step(records[pieces[strip]], strip, cells_of):
            state[strip, :, lanes] = cells[strip, :, lanes].astype(F32) + moved
    if loops:
        lax.fori_loop(1, chunks, more_cells(ranks, table, cells_of), 0)


    def split_cells(strip, lanes):
        high, low = split(state[strip, :, lanes])
        if loops:
            source[strip, :MEMBERS, lanes] = high
            source[strip, MEMBERS:, lanes] = low
        return jnp.concatenate([high, high, low], axis=0)

    def source_of(strip, lanes):
        high = source[strip, :MEMBERS, lanes]
        return jnp.concatenate([high, high, source[strip, MEMBERS:, lanes]], axis=0)

    for strip in range(STRIPS):
        for lanes, moved in region_step(records_1[pieces[strip]], strip, split_cells):
            if loops:
                state[strip, :, lanes] = state[strip, :, lanes] + moved
                continue
            done = state[strip, :, lanes] + moved
            for line in range(ROWS):
                place = pl.ds(lanes.start // STRIP + line, MEMBERS, stride=LINES)
                wide[strip, place, :] = done[:, line * STRIP : (line + 1) * STRIP]
        if not loops:
            message_ref[:, strip * STRIP : (strip + 1) * STRIP] = wide[strip].astype(BF16)
    if loops:
        lax.fori_loop(1, chunks_1, more_cells(ranks_1, table_1, source_of), 0)
        for strip in range(STRIPS):
            for line in range(LINES):
                wide[strip, pl.ds(line, MEMBERS, stride=LINES), :] = state[strip, :, pl.ds(line * STRIP, STRIP)]
            message_ref[:, strip * STRIP : (strip + 1) * STRIP] = wide[strip].astype(BF16)
    return (jnp.maximum(chunks, chunks_1) > 1) | (site_chunks > 1)


def call(kernel, shape, operands, scratch=(), scalars=0, flops=0, moved=1 << 18):
    smem = pl.BlockSpec(memory_space=pltpu.SMEM)
    vmem = pl.BlockSpec(memory_space=pltpu.VMEM)
    return pl.pallas_call(
        kernel,
        out_shape=jax.ShapeDtypeStruct(shape, BF16),
        in_specs=[smem if index < scalars else vmem for index in range(len(operands))],
        out_specs=vmem,
        scratch_shapes=list(scratch),
        compiler_params=pltpu.CompilerParams(vmem_limit_bytes=VMEM_LIMIT),
        cost_estimate=pl.CostEstimate(flops=flops, bytes_accessed=moved, transcendentals=0),
    )(*operands)


MESSAGE = (MEMBERS * LINES, HALF)


def pack(field):
    return call(pack_kernel, MESSAGE, (field,), moved=1 << 20)


def unpack(message):
    return call(unpack_kernel, (LEVELS, CHIPS * ROWS, SPAN_EAST), (message,), moved=1 << 20)


def state_facts(place, datum, noise, point, count):
    smem = pl.BlockSpec(memory_space=pltpu.SMEM)
    vmem = pl.BlockSpec(memory_space=pltpu.VMEM)
    return pl.pallas_call(
        facts_kernel,
        out_shape=jax.ShapeDtypeStruct((FACTS, 2 * SLOTS), BF16),
        in_specs=[smem, vmem, vmem, vmem, smem],
        out_specs=vmem,
        compiler_params=pltpu.CompilerParams(vmem_limit_bytes=VMEM_LIMIT),
    )(place, datum, noise, point, count)


def choose(place, own, other):
    smem = pl.BlockSpec(memory_space=pltpu.SMEM)
    vmem = pl.BlockSpec(memory_space=pltpu.VMEM)
    return pl.pallas_call(
        choose_kernel,
        out_shape=[jax.ShapeDtypeStruct((rows, 4 * SLOTS), BF16) for rows in (HALF, FACTS)],
        in_specs=[smem, vmem, vmem],
        out_specs=[vmem, vmem],
        compiler_params=pltpu.CompilerParams(vmem_limit_bytes=VMEM_LIMIT),
    )(place, own, other)


def pick(place, field, chooser, facts):
    scratch = [pltpu.VMEM((2, MEMBERS * LINES, 2 * SLOTS), F32)]
    return call(
        pick_kernel, (PACKET, 4 * SLOTS), (place, field, chooser, facts), scratch, 1, 1 << 27, 1 << 19
    )


def merge(place, own, other, beyond):
    smem = pl.BlockSpec(memory_space=pltpu.SMEM)
    vmem = pl.BlockSpec(memory_space=pltpu.VMEM)
    lanes = (2 * BATCH_LANES, BATCH_LANES + 2 * SLOTS, BATCH_LANES + 2 * SLOTS)
    return pl.pallas_call(
        merge_kernel,
        out_shape=[jax.ShapeDtypeStruct((PACKET, count), BF16) for count in lanes],
        in_specs=[smem, vmem, vmem, vmem],
        out_specs=[vmem, vmem, vmem],
        compiler_params=pltpu.CompilerParams(vmem_limit_bytes=VMEM_LIMIT),
        cost_estimate=pl.CostEstimate(flops=0, bytes_accessed=1 << 18, transcendentals=0),
    )(place, own, other, beyond)


def arrange(field):
    scratch = [pltpu.VMEM((STRIPS, MEMBERS * LINES, STRIP), F32)]
    return call(arrange_kernel, (STRIPS, MEMBERS, LINES * STRIP), (field,), scratch, moved=1 << 20)


def analyse(place, cells, first, here, second):
    scratch = [
        pltpu.VMEM((STRIPS, MEMBERS * LINES, STRIP), F32),
        pltpu.VMEM((STRIPS, MEMBERS, LINES * STRIP), F32),
        pltpu.VMEM((STRIPS, 2 * MEMBERS, LINES * STRIP), BF16),
        pltpu.VMEM((MEMBERS, 2 * BATCH_LANES), F32),
    ]
    return call(
        analysis_kernel, MESSAGE, (place, cells, first, here, second), scratch, 1, 1 << 30, 1 << 20
    )


def swap_cores(block):
    return lax.ppermute(block, "mem", [(i, i ^ 1) for i in range(lax.axis_size("mem"))])


def swap_beyond(block):
    rows, columns = lax.axis_size("mem"), lax.axis_size("tile")
    route = []
    for row in range(0, rows, 2):
        for column in range(columns - 1):
            west, east = (row + 1) * columns + column, row * columns + column + 1
            route += [(west, east), (east, west)]
    return lax.ppermute(block, ("mem", "tile"), route)


def swap_regions(block, start):
    route = []
    for region in range(start, CHIPS - 1, 2):
        for half in range(2):
            one, two = 2 * region + half, 2 * region + 2 + half
            route += [(one, two), (two, one)]
    return lax.ppermute(block, "mem", route)


def on_device(members, datum, noise, point, count):
    row = lax.axis_index("mem")
    column = lax.axis_index("tile")
    half = row % 2
    region = row // 2
    place = jnp.stack(
        [
            row * SPAN_NORTH,
            column * SPAN_EAST,
            half,
            region * ROWS,
            column * SPAN_EAST + half * HALF,
            region % 2,
        ]
    ).astype(jnp.int32)
    message = pack(members[0])
    field = lax.all_to_all(message, "mem", split_axis=0, concat_axis=0, tiled=True)
    facts = state_facts(place, datum, noise, point, count.reshape(2))
    chooser, facts = choose(place, facts, swap_cores(facts))
    packet = pick(place, field, chooser, facts)
    field, packet = lax.optimization_barrier((field, packet))
    beyond = swap_beyond(packet)
    other = swap_cores(packet)
    cells, other, beyond = lax.optimization_barrier((arrange(field), other, beyond))
    here, first, second = merge(place, packet, other, beyond)
    first, second = swap_regions(first, 0), swap_regions(second, 1)
    message = analyse(place, cells, first, here, second)
    message = lax.all_to_all(message, "mem", split_axis=0, concat_axis=0, tiled=True)
    return unpack(message)[None]


def solution(mesh):
    return jax.shard_map(
        on_device,
        mesh=mesh,
        in_specs=(
            P("mem", None, None, "tile"),
            P(None, "mem", "tile", None),
            P(None, "mem", "tile", None),
            P(None, "mem", "tile", None),
            P(None, "mem", "tile"),
        ),
        out_specs=P("mem", None, None, "tile"),
        check_vma=False,
    )
```
